256 devices in a mesh: blk: 8 (over x, core), row: 32 (over z, y).
Axes of the slice: x: 4, y: 4, z: 8, core: 2. Of those that a mesh axis runs over, the one named last changes fastest.
Arguments:
- dyn_state: float32 [4, 72, 128, 256], P(None, None, 'blk', 'row'), may hold values from -6 to 6
- crm_state: bfloat16 [3, 58, 524288], P(None, None, ('blk', 'row')), may hold values from -6 to 6
- cloud_mask: int32 [58, 524288], P(None, ('blk', 'row')), may hold values 0 or 1
- span_of: int32 [8192, 1], P(('blk', 'row')), may hold values from 0 to 31; in each aligned block of 32 rows (0 to 31, 32 to 63, ...) at most 2 rows name the same one
Outputs:
- dyn_out: float32 [4, 72, 128, 256], P(None, None, 'blk', 'row')
- crm_out: bfloat16 [3, 58, 524288], P(None, None, ('blk', 'row'))
The draws below stay inside these ranges and needn't reach their ends.
Inputs may be any that keep to these rules, and one draw needn't show every extreme that they name: `span_of`: within the 32 columns of one device at most 2 name the same span, a bound that some block reaches.
All inputs are finite; a program needn't handle non-finite values. No bound on the sum of `cloud_mask` on one device may be relied on, other than what follows from the above.
Results may differ from the reference program's by a relative error of at most 0.001.
Values sent between devices are 32-bit elements; how exact they have to be, the bound alone decides.
A program may use at most 128 MiB of HBM per device.

```python
import math
import jax
import jax.numpy as jnp
import numpy as np
from jax import lax

LEV = 72
CRM_LEV = 58
CRM_COLS = 32
SUBSTEPS = 2
EX_DEV = 4
EY_DEV = 2
COL_DEV = 32
SLOT_DEV = 64
CAP = 2
COLUMNS = 8192
NXN = 128
NYN = 256
CRM_CELLS = 524288
N_BLK = 8
N_ROW = 32


def place_ends(entries, own_key, least, largest):
    dims = entries.shape
    index_at = [jax.random.randint(jax.random.fold_in(own_key, axis), (), 0, dims[axis]) for axis in range(len(dims))]
    entries = entries.at[tuple(index_at)].set(least)
    longest = dims.index(max(dims))
    index_at[longest] = (index_at[longest] + 1) % dims[longest]
    return entries.at[tuple(index_at)].set(largest)


def shard_levels(key, dims, split, smallest, largest):
    def one(position, shards_of):
        draws = jax.random.uniform(jax.random.fold_in(jax.random.fold_in(key, 6), position), (shards_of,), jnp.float32, smallest / len(split), largest / len(split))
        return jnp.repeat(jnp.exp(draws), dims[position] // shards_of).reshape((-1,) + (1,) * (len(dims) - position - 1))

    gain = one(*split[0])
    for cut in split[1:]:
        gain = gain * one(*cut)
    return gain


def deal_out(own_key, own, number, rows, count, top, most, lean):
    sequence = jax.random.permutation(own_key, count)
    heavy_load, ordinary = load_shares(count, rows * top, most, lean, True), load_shares(count, rows * top, most, lean, False)
    places = jnp.arange(count)

    def named(sizes, offset_by):
        used = int((sizes > 0).sum())
        fixed = max(1, used // 4)
        passed = fixed + (places - fixed + offset_by * (used - fixed)) % max(1, count - fixed)
        return jnp.zeros((count,), jnp.int32).at[sequence[jnp.where(places < fixed, places, passed)]].set(jnp.asarray(sizes, jnp.int32))

    sizes = jnp.where(number % 4 == 0, named(heavy_load, number // 4), named(ordinary, number - number // 4 - 1))
    mixed = jax.random.permutation(jax.random.fold_in(own, 3), count)
    donor, receiver = mixed[0:count // 2 * 2:2], mixed[1:count // 2 * 2:2]
    margin = jnp.minimum(sizes[donor] - 1, most - sizes[receiver]) // 2
    margin = jnp.where((donor == sequence[0]) | (receiver == sequence[0]) | (sizes[receiver] == 0), 0, jnp.maximum(margin, 0))
    passed = jax.random.randint(jax.random.fold_in(own, 4), (count // 2,), 0, 1 << 20) % (margin + 1)
    sizes = sizes.at[donor].add(-passed).at[receiver].add(passed)
    members = jnp.searchsorted(jnp.cumsum(sizes), jnp.arange(rows * top), side="right").astype(jnp.int32)
    table = members.reshape(top, rows).T
    table = table[jax.random.permutation(jax.random.fold_in(own, 1), rows)]
    offset_by = jax.random.randint(jax.random.fold_in(own, 2), (rows, 1), 0, top)
    return jnp.take_along_axis(table, (jnp.arange(top)[None, :] + offset_by) % top, axis=1)


def load_shares(amount, total, reach, slope, full):
    weights = [(1 << 20) // math.isqrt(grade ** slope) + 1 for grade in range(1, amount + 1)]
    largest = reach if full else min(reach, max(-(-total // amount), total * weights[0] // sum(weights)))
    least = 1 if total - largest >= amount - 1 else 0
    counts, rest = [largest] + [least] * (amount - 1), total - largest - least * (amount - 1)
    while rest > 0:
        movable = [i for i in range(1, amount) if counts[i] < largest] or [i for i in range(1, amount) if counts[i] < reach]
        pool, remaining = sum([weights[i] for i in movable]), rest
        for i in movable:
            extra = min(reach - counts[i], max(1, remaining * weights[i] // pool), rest)
            counts[i] = counts[i] + extra
            rest = rest - extra
    return np.array(counts)


def noise(key, shape, scale, reach, shards=(), kind=jnp.bfloat16):
    gain = shard_levels(key, shape, shards, -0.22, 0.18) if shards else 1.0
    result = jax.random.normal(key, shape, jnp.float32) * scale * gain
    return jnp.minimum(jnp.maximum(result, -reach), reach).astype(kind)


def setup_inputs(seed: int = 0) -> dict:
    streams_of = jax.random.split(jax.random.key(seed), 5)
    dyn_state = noise(streams_of[0], (4, LEV, NXN, NYN), 1.0, 6.0, ((2, 8), (3, 32)), jnp.float32)
    crm_state = noise(streams_of[1], (3, CRM_LEV, CRM_CELLS), 1.0, 6.0, ((2, 256),))
    cloud_mask = place_ends((jax.random.randint(streams_of[2], (CRM_LEV, CRM_CELLS), 0, 3) < 1).astype(jnp.int32), jax.random.fold_in(streams_of[2], 1), 0, 1)
    span_of_keys = jax.random.split(jax.random.fold_in(streams_of[3], 1), COLUMNS // COL_DEV)
    span_of_turns = jax.random.permutation(jax.random.fold_in(streams_of[3], 3), COLUMNS // COL_DEV)
    span_of = jax.vmap(lambda own, number: deal_out(jax.random.fold_in(streams_of[3], 2), own, number, COL_DEV, N_ROW, 1, CAP, 1))(span_of_keys, span_of_turns).reshape((COLUMNS, 1))
    return dict(dyn_state=dyn_state, crm_state=crm_state, cloud_mask=cloud_mask, span_of=span_of)


def poly_times(first_poly, second_poly):
    product = [0.0] * (len(first_poly) + len(second_poly) - 1)
    for first_index in range(len(first_poly)):
        for second_index in range(len(second_poly)):
            product[first_index + second_index] += first_poly[first_index] * second_poly[second_index]
    return product

def poly_slope(coeffs, point):
    result_value = 0.0
    for power in range(1, len(coeffs)):
        result_value += power * coeffs[power] * point ** (power - 1)
    return result_value

def poly_integral(coeffs, lower_end, upper_end):
    result_value = 0.0
    for power in range(len(coeffs)):
        result_value += coeffs[power] * (upper_end ** (power + 1) - lower_end ** (power + 1)) / (power + 1)
    return result_value

def element_tables():
    root_five = float(np.sqrt(5.0))
    gll_nodes = [-1.0, -1.0 / root_five, 1.0 / root_five, 1.0]
    weights = np.array([1.0 / 6.0, 5.0 / 6.0, 5.0 / 6.0, 1.0 / 6.0])
    derivative = np.zeros((4, 4))
    to_cells = np.zeros((2, 4))
    for basis in range(4):
        coeffs = [1.0]
        for other in range(4):
            if other != basis:
                denominator = gll_nodes[basis] - gll_nodes[other]
                coeffs = poly_times(coeffs, [-gll_nodes[other] / denominator, 1.0 / denominator])
        for node in range(4):
            derivative[node, basis] = poly_slope(coeffs, gll_nodes[node])
        to_cells[0, basis] = poly_integral(coeffs, -1.0, 0.0)
        to_cells[1, basis] = poly_integral(coeffs, 0.0, 1.0)
    to_nodes = np.array([[1.0, 0.0], [1.0, 0.0], [0.0, 1.0], [0.0, 1.0]])
    edge_weights = np.array([1.0 / 3.0, 5.0 / 6.0, 5.0 / 6.0, 1.0 / 3.0])
    return (derivative, weights, to_cells, to_nodes, edge_weights)

def slot_mean(field, ncols):
    return field.reshape(field.shape[0], -1, ncols).mean(axis=2)

def spread(profile, ncols):
    return jnp.repeat(profile, ncols, axis=1)

def transport(field, momentum, ncols):
    column = lax.broadcasted_iota(jnp.int32, field.shape, 1) % ncols
    east = jnp.where(column == ncols - 1, jnp.roll(field, ncols - 1, axis=1), jnp.roll(field, -1, axis=1))
    west = jnp.where(column == 0, jnp.roll(field, 1 - ncols, axis=1), jnp.roll(field, 1, axis=1))
    upper = jnp.concatenate([field[1:], field[-1:]], axis=0)
    lower = jnp.concatenate([field[:1], field[:-1]], axis=0)
    return field - 0.2 * momentum * (east - west) * 0.5 + 0.15 * (east - 2.0 * field + west) + 0.15 * (upper - 2.0 * field + lower)

def crm_substep(fields, forcing, wet, saturation, ncols):
    momentum = fields[2]
    moved = []
    for field, target in zip(fields, forcing):
        moved.append(transport(field, momentum, ncols) + 0.3 * spread(target - slot_mean(field, ncols), ncols))
    heat, water, motion = moved
    condensed = wet * 0.5 * jnp.maximum(water - 0.5 * heat - saturation, 0.0)
    return (heat + 0.8 * condensed, water - condensed, motion)

def cloud_model(state, profiles, cloud_mask, ncols):
    levels = state.shape[1]
    start = tuple((state[k].astype(jnp.float32) for k in range(3)))
    forcing = tuple((profiles[k, :levels] for k in range(3)))
    wet = cloud_mask.astype(jnp.float32)
    saturation = (0.5 - jnp.arange(levels, dtype=jnp.float32) / levels)[:, None]
    fields = start
    for substep in range(SUBSTEPS):
        fields = crm_substep(fields, forcing, wet, saturation, ncols)
    final = jnp.stack(fields).astype(jnp.bfloat16)
    change = jnp.stack([slot_mean(fields[k] - start[k], ncols) for k in range(3)])
    tendency = jnp.pad(change, ((0, 0), (0, profiles.shape[1] - levels), (0, 0)))
    return (final, tendency)

def edge_fold(field):
    node_x = (jnp.arange(field.shape[2]) % 4)[:, None]
    field = field + jnp.where(node_x == 0, jnp.roll(field, 1, axis=2), 0.0) + jnp.where(node_x == 3, jnp.roll(field, -1, axis=2), 0.0)
    node_along = jnp.arange(field.shape[3]) % 4
    return field + jnp.where(node_along == 0, jnp.roll(field, 1, axis=3), 0.0) + jnp.where(node_along == 3, jnp.roll(field, -1, axis=3), 0.0)

def reference(dyn_state, crm_state, cloud_mask, span_of):
    derivative, weights, to_cells, to_nodes, edge_weights = element_tables()
    highest = lax.Precision.HIGHEST
    derivative = jnp.asarray(derivative, jnp.float32)
    weight_vec = jnp.asarray(weights, jnp.float32)
    cell_table = jnp.asarray(to_cells, jnp.float32)
    node_table = jnp.asarray(to_nodes, jnp.float32)
    groups = N_BLK * N_ROW
    grid = dyn_state[:3].reshape(3, LEV, N_BLK, EX_DEV, 4, N_ROW, EY_DEV, 4)
    cells = jnp.einsum('ai,bj,flxuiyej->flxyuaeb', cell_table, cell_table, grid, precision=highest)
    column_state = cells.reshape(3, LEV, N_BLK, N_ROW, COL_DEV).transpose(2, 3, 4, 0, 1)
    span_index = span_of[:, 0].reshape(N_BLK, N_ROW, COL_DEV)
    match = (span_index[..., None] == jnp.arange(N_ROW, dtype=jnp.int32)).astype(jnp.int32)
    earlier = jnp.cumsum(match, axis=2) - match
    within = lax.optimization_barrier(jnp.sum(earlier * match, axis=3))
    source = jnp.arange(N_ROW, dtype=jnp.int32)[None, :, None]
    target = (source * CAP + within).astype(jnp.int32)
    block_index = jnp.broadcast_to(jnp.arange(N_BLK, dtype=jnp.int32)[:, None, None], span_index.shape)
    inbox = jnp.zeros((N_BLK, N_ROW, SLOT_DEV, 3, LEV), jnp.float32)
    inbox = inbox.at[block_index, span_index, target].set(column_state)
    profiles = inbox.reshape(groups, SLOT_DEV, 3, LEV).transpose(0, 2, 3, 1)
    states = crm_state.reshape(3, CRM_LEV, groups, SLOT_DEV * CRM_COLS).transpose(2, 0, 1, 3)
    masks = cloud_mask.reshape(CRM_LEV, groups, SLOT_DEV * CRM_COLS).transpose(1, 0, 2)

    def one_device(packed):
        return cloud_model(packed[0], packed[1], packed[2], CRM_COLS)
    final, tendency = lax.map(one_device, (states, profiles, masks))
    crm_out = final.transpose(1, 2, 0, 3).reshape(3, CRM_LEV, groups * SLOT_DEV * CRM_COLS)
    per_span = tendency.reshape(N_BLK, N_ROW, 3, LEV, SLOT_DEV)
    column_tendency = per_span[block_index, span_index, :, :, target]
    column_tendency = column_tendency.transpose(3, 4, 0, 1, 2).reshape(3, LEV, N_BLK, N_ROW, EX_DEV, 2, EY_DEV, 2)
    node_tendency = jnp.einsum('ia,jb,flxyuaeb->flxuiyej', node_table, node_table, column_tendency, precision=highest)
    node_tendency = node_tendency.reshape(3, LEV, NXN, NYN)
    raw = jnp.concatenate([dyn_state[:3] + node_tendency, dyn_state[3:]], axis=0)
    mass = jnp.asarray(np.outer(np.tile(weights, N_BLK * EX_DEV), np.tile(weights, N_ROW * EY_DEV)), jnp.float32)
    total = jnp.asarray(np.outer(np.tile(edge_weights, N_BLK * EX_DEV), np.tile(edge_weights, N_ROW * EY_DEV)), jnp.float32)
    state_one = edge_fold(mass * raw) / total
    shaped = state_one.reshape(4, LEV, N_BLK * EX_DEV, 4, N_ROW * EY_DEV, 4)
    gradient_x = jnp.einsum('km,flxmyj->flxkyj', derivative, shaped, precision=highest)
    contrib_x = -jnp.einsum('ki,k,j,flxkyj->flxiyj', derivative, weight_vec, weight_vec, gradient_x, precision=highest)
    gradient_y = jnp.einsum('km,flxiym->flxiyk', derivative, shaped, precision=highest)
    contrib_y = -jnp.einsum('kj,i,k,flxiyk->flxiyj', derivative, weight_vec, weight_vec, gradient_y, precision=highest)
    contrib = (contrib_x + contrib_y).reshape(4, LEV, NXN, NYN)
    dyn_out = state_one + 0.01 * edge_fold(contrib) / total
    return (dyn_out, crm_out)
```

```python
import functools

import jax
import jax.numpy as jnp
import numpy as np
from jax import lax
from jax.experimental import pallas as pl
from jax.experimental.pallas import tpu as pltpu
from jax.sharding import PartitionSpec as P

MESH = pl.DeviceIdType.MESH
LEV, CRM_LEV, CRM_COLS = 72, 58, 32
F32, BF16 = jnp.float32, jnp.bfloat16
SLOTS = ((0, -1), (0, 1), (-1, 0), (1, 0), (-1, -1), (-1, 1), (1, -1), (1, 1))
STATE_ROWS = (32, 32, 16, 16, 8, 8, 8, 8)
CELL_ROWS = (24, 24, 16, 16, 8, 8, 8, 8)
STATE_AT = tuple(int(v) for v in np.cumsum((0,) + STATE_ROWS))
CELL_AT = tuple(int(v) for v in np.cumsum((0,) + CELL_ROWS))
HALO = CELL_AT[-1]
CELLS = 32 + HALO


def poly_times(first_poly, second_poly):
    product = [0.0] * (len(first_poly) + len(second_poly) - 1)
    for i, first in enumerate(first_poly):
        for j, second in enumerate(second_poly):
            product[i + j] += first * second
    return product


def poly_slope(coeffs, point):
    return sum(power * coeffs[power] * point ** (power - 1) for power in range(1, len(coeffs)))


def poly_integral(coeffs, low, high):
    return sum(
        coeffs[power] * (high ** (power + 1) - low ** (power + 1)) / (power + 1)
        for power in range(len(coeffs))
    )


def element_tables():
    root_five = float(np.sqrt(5.0))
    gll_nodes = [-1.0, -1.0 / root_five, 1.0 / root_five, 1.0]
    weights = np.array([1.0 / 6.0, 5.0 / 6.0, 5.0 / 6.0, 1.0 / 6.0])
    derivative = np.zeros((4, 4))
    to_cells = np.zeros((2, 4))
    for basis in range(4):
        coeffs = [1.0]
        for other in range(4):
            if other != basis:
                denominator = gll_nodes[basis] - gll_nodes[other]
                coeffs = poly_times(coeffs, [-gll_nodes[other] / denominator, 1.0 / denominator])
        for node in range(4):
            derivative[node, basis] = poly_slope(coeffs, gll_nodes[node])
        to_cells[0, basis] = poly_integral(coeffs, -1.0, 0.0)
        to_cells[1, basis] = poly_integral(coeffs, 0.0, 1.0)
    to_nodes = np.array([[1.0, 0.0], [1.0, 0.0], [0.0, 1.0], [0.0, 1.0]])
    edge_weights = np.array([1.0 / 3.0, 5.0 / 6.0, 5.0 / 6.0, 1.0 / 3.0])
    return derivative, weights, to_cells, to_nodes, edge_weights


def line_operators(elements):
    derivative, weights, _, _, edge_weights = element_tables()
    count = elements * 4 * 3
    weight = np.tile(weights, elements * 3)
    fold = np.eye(count)
    for node in range(count):
        if node % 4 == 0:
            fold[node, (node - 1) % count] += 1.0
        if node % 4 == 3:
            fold[node, (node + 1) % count] += 1.0
    fold = fold / np.tile(edge_weights, elements * 3)[:, None]
    smooth = fold * weight
    stiff = np.kron(np.eye(elements * 3), derivative.T @ np.diag(weights) @ derivative)
    mine = slice(elements * 4, elements * 8)
    return smooth[mine], (fold @ stiff @ smooth)[mine], (smooth @ smooth)[mine]


def split(value):
    high = np.asarray(value, np.float32).astype(jnp.bfloat16)
    return high, (np.asarray(value, np.float32) - high.astype(np.float32)).astype(jnp.bfloat16)


@functools.cache
def tables():
    _, _, to_cells, to_nodes, _ = element_tables()
    smooth_x, stiff_x, mass_x = line_operators(4)
    smooth_y, stiff_y, mass_y = line_operators(2)
    nodes = np.kron(np.kron(np.eye(4), to_nodes), np.kron(np.eye(2), to_nodes))

    def block(dx, dy):
        x, y = slice(16 * (dx + 1), 16 * (dx + 2)), slice(8 * (dy + 1), 8 * (dy + 2))
        return np.kron(smooth_x[:, x], smooth_y[:, y]) - 0.01 * (
            np.kron(stiff_x[:, x], mass_y[:, y]) + np.kron(mass_x[:, x], stiff_y[:, y])
        )

    cell_sums = np.zeros((32, 128))
    cell_sums[:] = np.kron(np.kron(np.eye(4), to_cells), np.kron(np.eye(2), to_cells))
    mine = block(0, 0)
    own = np.zeros((128, 128))
    own[:, :32] = mine @ nodes
    outer, inner = np.zeros((128, 128)), np.zeros((128, 128))
    halo = np.zeros((128, 128))
    pick = np.zeros((CELLS, 128), np.float32)
    pick[:32, :32] = np.eye(32)
    for slot, (dx, dy) in enumerate(SLOTS):
        part = block(dx, dy)
        left, scale, right = np.linalg.svd(part)
        rank = int((scale > 1e-10).sum())
        assert rank <= STATE_ROWS[slot]
        at = STATE_AT[slot]
        outer[:, at : at + rank] = left[:, :rank] * np.sqrt(scale[:rank])
        inner[at : at + rank] = right[:rank] * np.sqrt(scale[:rank])[:, None]
        cells = part @ nodes
        used = np.flatnonzero(np.abs(cells).max(axis=0) > 1e-12)
        assert len(used) <= CELL_ROWS[slot]
        at = CELL_AT[slot]
        halo[:, at : at + len(used)] = cells[:, used]
        pick[32 + at + np.arange(len(used)), used] = 1.0
    pieces = []
    for matrix in (cell_sums, inner, mine, outer, own, halo):
        pieces.extend(split(matrix))
    matrices = np.concatenate(pieces, axis=0)

    cell = np.arange(128)
    same = (cell[:, None] // 32) == (cell[None, :] // 32)
    step = (cell[:, None] - cell[None, :]) % 32
    east, west = same & (step == 1), same & (step == 31)
    along = np.concatenate([1.0 * east + 1.0 * west - same / 16.0, 1.0 * east - 1.0 * west], axis=1)
    along = np.concatenate([along, along], axis=0).astype(jnp.bfloat16)

    spread = np.zeros((128, 384))
    for s in range(2):
        for pair in range(2):
            for field in range(3):
                at = field * 128 + pair * 64 + s * 32
                spread[s * 8 + pair * 4 + field, at : at + 32] = 1.0
    means = (spread[:16] / 32.0).astype(jnp.bfloat16)
    spread = np.concatenate([spread, spread], axis=0).astype(jnp.bfloat16)
    return matrices, along, spread, means, pick


def halves(value):
    high = value.astype(BF16)
    return high, (value - high.astype(F32)).astype(BF16)


def dot(left, right):
    return jnp.dot(left, right, preferred_element_type=F32)


def dot_split(left, right):
    high, low = halves(right)
    return dot(left[0], high) + dot(left[1], high) + dot(left[0], low)


def iota(shape, axis):
    return lax.broadcasted_iota(jnp.int32, shape, axis)


def levels_moved(field, row):
    up = jnp.where(row == CRM_LEV - 1, field, pltpu.roll(field, 63, 0))
    down = jnp.where(row == 0, field, pltpu.roll(field, 1, 0))
    return up + down


def transported(field, along, momentum, row):
    return (
        0.4 * field
        + 0.15 * (along[:, :128] + levels_moved(field, row))
        + momentum * along[:, 128:]
    )


def condensed(heat, water, wet, saturation):
    cond = wet * jnp.maximum(water - 0.5 * heat - saturation, 0.0)
    return heat + 0.8 * cond, water - cond


def kernel(
    dyn, crm, mask, span, matrices, along_in, spread_in, means_in, pick_in,
    dyn_out, crm_out,
    xin, xb, mk, sp, mat, along, spread, means, pick,
    spans, xs, ys, wt, cat, og, ar, rs, rt, dh, dr, hs, hr, ob, od, place,
    load_sem, store_sem, go_sem, come_sem,
):
    p, r = lax.axis_index("blk"), lax.axis_index("row")
    rows, blocks = lax.axis_size("row"), lax.axis_size("blk")
    loads = [
        pltpu.make_async_copy(source, target, load_sem.at[k])
        for k, (source, target) in enumerate(
            ((span, sp), (dyn, xin), (matrices, mat), (pick_in, pick), (along_in, along),
             (crm, xb), (mask, mk), (spread_in, spread), (means_in, means))
        )
    ]
    for load in loads:
        load.start()

    barrier = pltpu.get_barrier_semaphore()

    def greet(k, carry):
        pl.semaphore_signal(
            barrier, inc=1, device_id=(p, lax.rem(r + k, rows)), device_id_type=MESH
        )
        return carry

    lax.fori_loop(1, rows, greet, None)
    around = [
        (lax.rem(p + blocks - dx, blocks), lax.rem(r + rows - dy, rows)) for dx, dy in SLOTS
    ]
    for slot in range(2, 8):
        pl.semaphore_signal(barrier, inc=1, device_id=around[slot], device_id_type=MESH)

    xs[...] = jnp.zeros_like(xs)
    wt[...] = jnp.zeros_like(wt)
    cat[...] = jnp.zeros_like(cat)
    spans[...] = jnp.zeros_like(spans)
    hr[HALO:128, :] = jnp.zeros((128 - HALO, 384), F32)

    def table(k, lines=128):
        at = (0, 64, 320, 576, 832, 1088)[k]
        return mat[at : at + lines], mat[at + lines : at + 2 * lines]

    loads[0].wait()
    spans[0:1, 0:32] = sp[...].astype(F32)
    named = spans[...]
    named = named + pltpu.roll(named, 32, 1)
    named = named + pltpu.roll(named, 64, 1)
    lane, line = iota((32, 128), 1), iota((32, 128), 0)
    across = jnp.broadcast_to(named[0:1, :], (32, 128))
    down = jnp.sum(jnp.where(lane == line, across, 0.0), axis=1, keepdims=True)
    earlier = jnp.where((down == across) & (line < (lane & 31)), 1.0, 0.0)
    position = 2.0 * named[0:1, :] + jnp.sum(earlier, axis=0, keepdims=True)
    lane, line = iota((128, 128), 1), iota((128, 128), 0)
    wanted = (2 * line - (line & 3)).astype(F32)
    offered = 4.0 * jnp.broadcast_to(position, (128, 128)) + (lane >> 5).astype(F32)
    send_to = jnp.concatenate(
        [jnp.where(offered - 4.0 * s == wanted, 1.0, 0.0) for s in range(2)], axis=1
    ).astype(BF16)

    loads[1].wait()
    loads[2].wait()
    for field in range(3):
        cat[32 * field : 32 * field + 32, 0:LEV] = dot_split(table(0, 32), xin[field])
    first = jnp.where(lane < CRM_LEV, cat[...], 0.0)
    high, low = halves(jnp.concatenate([first, pltpu.roll(first, 64, 1)], axis=0))
    sent = dot(send_to, jnp.concatenate([high, low], axis=1))
    og[...] = (sent[:, :128] + sent[:, 128:]).reshape(32, 4, 128)

    pl.semaphore_wait(barrier, rows - 1 + 6)

    def profile_copy(target):
        return pltpu.make_async_remote_copy(
            src_ref=og.at[target], dst_ref=ar.at[r], send_sem=go_sem.at[0],
            recv_sem=come_sem.at[0], device_id=(p, target), device_id_type=MESH,
        )

    def send_profile(k, carry):
        away = 16 + (1 - 2 * (k & 1)) * ((k + 1) >> 1)
        profile_copy(lax.rem(r + away, rows)).start()
        return carry

    lax.fori_loop(0, rows - 1, send_profile, None)
    ar[r] = og[r]

    for field in range(4):
        dh[:, 128 * field : 128 * field + LEV] = dot_split(table(1), xin[field])
    state_copies = []
    for slot in range(8):
        at = pl.ds(STATE_AT[slot], STATE_ROWS[slot])
        state_copies.append(
            pltpu.make_async_remote_copy(
                src_ref=dh.at[at], dst_ref=dr.at[at], send_sem=go_sem.at[1],
                recv_sem=come_sem.at[1], device_id=around[slot], device_id_type=MESH,
            )
        )
        state_copies[-1].start()

    for k in range(4, 9):
        loads[k].wait()
    row = iota((64, 128), 0)
    saturation = 0.5 - row.astype(F32) / CRM_LEV

    def begin(j, carry):
        at = pl.ds(pl.multiple_of(j * 128, 128), 128)
        for field in range(3):
            xs[j, 64 * field : 64 * field + CRM_LEV, :] = xb[field, :, at].astype(F32)
        wt[j, 0:CRM_LEV, :] = 0.5 * mk[:, at].astype(F32)
        state = xs[j]
        shifted = dot(state.astype(BF16), along[0:128, :])
        momentum = -0.1 * state[128:192]
        for field in range(3):
            part = slice(64 * field, 64 * field + 64)
            ys[j, part, :] = transported(state[part], shifted[part], momentum, row)
        return carry

    lax.fori_loop(0, 16, begin, None, unroll=2)

    for field in range(4):
        od[field] = dot_split(table(2), xin[field])

    loads[3].wait()
    back = jnp.sum(pick[...] * jnp.broadcast_to(position, (CELLS, 128)), axis=1, keepdims=True)
    lane = iota((CELLS, 128), 1)
    code = (2 * lane - (lane & 3)).astype(F32)
    for field in range(3):
        place[field] = jnp.concatenate(
            [jnp.where(4.0 * back + field - 4.0 * s == code, 1.0, 0.0) for s in range(2)], axis=1
        ).astype(BF16)

    def all_of(source, target, k):
        return pltpu.make_async_remote_copy(
            src_ref=source.at[pl.ds(0, 31)], dst_ref=target.at[pl.ds(0, 31)],
            send_sem=go_sem.at[k], recv_sem=come_sem.at[k],
            device_id=(p, lax.rem(r + 1, rows)), device_id_type=MESH,
        )

    all_of(og, ar, 0).wait_recv()
    forcing = ar[...].reshape(128, 128).T

    def tendency_copy(target):
        return pltpu.make_async_remote_copy(
            src_ref=rs.at[target], dst_ref=rt.at[r], send_sem=go_sem.at[2],
            recv_sem=come_sem.at[2], device_id=(p, target), device_id_type=MESH,
        )

    def finish(k, carry):
        away = 8 + (1 - 2 * (k & 1)) * ((k + 1) >> 1)
        j = lax.rem((r >> 1) + away, 16)
        at = pl.ds(pl.multiple_of(j * 128, 128), 128)
        shift = lax.rem(128 - 8 * j, 128)
        lane = iota((64, 128), 1)
        near = jnp.where(
            lane < 8,
            pltpu.roll(forcing[0:64], shift, 1),
            pltpu.roll(forcing[64:128], lax.rem(shift + 8, 128), 1),
        )
        near = jnp.where(lane < 16, near, 0.0)
        pulled = 0.3 * dot(jnp.concatenate(halves(near), axis=1), spread[...])
        wet = wt[j]
        one = [
            ys[j, 64 * field : 64 * field + 64, :] + pulled[:, 128 * field : 128 * field + 128]
            for field in range(3)
        ]
        one[0], one[1] = condensed(one[0], one[1], wet, saturation)
        both = [jnp.concatenate(halves(value), axis=1) for value in one]
        shifted = dot(jnp.concatenate(both, axis=0), along[...])
        momentum = -0.1 * one[2]
        two = [
            transported(one[field], shifted[64 * field : 64 * field + 64], momentum, row)
            + pulled[:, 128 * field : 128 * field + 128]
            for field in range(3)
        ]
        two[0], two[1] = condensed(two[0], two[1], wet, saturation)
        change = []
        for field in range(3):
            ob[field, :, at] = two[field][0:CRM_LEV].astype(BF16)
            change.append(halves(two[field] - xs[j, 64 * field : 64 * field + 64, :]))
        change = jnp.concatenate(
            [jnp.concatenate([c[half] for c in change], axis=1) for half in range(2)], axis=0
        )
        mean = lax.dot_general(
            means[...], change, (((1,), (1,)), ((), ())), preferred_element_type=F32
        )
        mean = mean + pltpu.roll(mean, 64, 1)
        message = jnp.where(iota((8, 128), 1) < 64, mean[0:8], mean[8:16])
        for pair in range(2):
            target = 2 * j + pair
            rs[target] = message[4 * pair : 4 * pair + 4]

            @pl.when(target != r)
            def _():
                tendency_copy(target).start()

        return carry

    lax.fori_loop(0, 16, finish, None, unroll=2)
    rt[r] = rs[r]

    store = pltpu.make_async_copy(ob, crm_out, store_sem.at[0])
    store.start()

    pltpu.make_async_remote_copy(
        src_ref=dh, dst_ref=dr, send_sem=go_sem.at[1], recv_sem=come_sem.at[1],
        device_id=around[0], device_id_type=MESH,
    ).wait_recv()
    for field in range(4):
        od[field] += dot_split(table(3), dr[:, 128 * field : 128 * field + 128])[:, 0:LEV]

    all_of(rs, rt, 2).wait_recv()
    given = rt[...].reshape(128, 128)
    lane = iota((128, 128), 1)
    given = jnp.concatenate(
        [jnp.where(lane < CRM_LEV, value, 0.0) for value in (given, pltpu.roll(given, 64, 1))],
        axis=0,
    )
    given = jnp.concatenate(halves(given), axis=1)
    cells = []
    for field in range(3):
        taken = dot(place[field], given)
        cells.append(taken[:, :128] + taken[:, 128:])
        hs[:, 128 * field : 128 * field + 128] = cells[field][32:]
    cell_copies = []
    for slot in range(8):
        at = pl.ds(CELL_AT[slot], CELL_ROWS[slot])
        cell_copies.append(
            pltpu.make_async_remote_copy(
                src_ref=hs.at[at], dst_ref=hr.at[at], send_sem=go_sem.at[3],
                recv_sem=come_sem.at[3], device_id=around[slot], device_id_type=MESH,
            )
        )
        cell_copies[-1].start()
    own = table(4)
    own = own[0][:, 0:32], own[1][:, 0:32]
    for field in range(3):
        od[field] += dot_split(own, cells[field][0:32])[:, 0:LEV]

    halo_copy = pltpu.make_async_remote_copy(
        src_ref=hs, dst_ref=hr.at[pl.ds(0, HALO)], send_sem=go_sem.at[3],
        recv_sem=come_sem.at[3], device_id=around[0], device_id_type=MESH,
    )
    halo_copy.wait_recv()
    for field in range(3):
        od[field] += dot_split(table(5), hr[:, 128 * field : 128 * field + 128])[:, 0:LEV]
    final = pltpu.make_async_copy(od, dyn_out, store_sem.at[1])
    final.start()
    all_of(og, ar, 0).wait_send()
    all_of(rs, rt, 2).wait_send()
    pltpu.make_async_remote_copy(
        src_ref=dh, dst_ref=dr, send_sem=go_sem.at[1], recv_sem=come_sem.at[1],
        device_id=around[0], device_id_type=MESH,
    ).wait_send()
    halo_copy.wait_send()
    store.wait()
    final.wait()


def per_device(dyn_state, crm_state, cloud_mask, span_of):
    consts = tuple(jnp.asarray(value) for value in tables())
    vmem = pltpu.VMEM
    scratch = [
        vmem((4, 128, LEV), F32), vmem((3, CRM_LEV, 2048), BF16), vmem((CRM_LEV, 2048), jnp.int32),
        vmem((1, 32), jnp.int32),
    ]
    scratch += [vmem(value.shape, value.dtype) for value in consts]
    scratch += [
        vmem((8, 128), F32),
        vmem((16, 192, 128), F32), vmem((16, 192, 128), F32), vmem((16, 64, 128), F32),
        vmem((128, 128), F32),
        vmem((32, 4, 128), F32), vmem((32, 4, 128), F32),
        vmem((32, 4, 128), F32), vmem((32, 4, 128), F32),
        vmem((128, 512), F32), vmem((128, 512), F32),
        vmem((HALO, 384), F32), vmem((128, 384), F32),
        vmem((3, CRM_LEV, 2048), BF16), vmem((4, 128, LEV), F32),
        vmem((3, CELLS, 256), BF16),
        pltpu.SemaphoreType.DMA((9,)), pltpu.SemaphoreType.DMA((2,)),
        pltpu.SemaphoreType.DMA((4,)), pltpu.SemaphoreType.DMA((4,)),
    ]
    nodes = dyn_state.transpose(0, 2, 3, 1).reshape(4, 128, LEV)
    dyn, crm = pl.pallas_call(
        kernel,
        out_shape=(
            jax.ShapeDtypeStruct((4, 128, LEV), F32),
            jax.ShapeDtypeStruct((3, CRM_LEV, 2048), BF16),
        ),
        in_specs=[pl.BlockSpec(memory_space=pl.ANY)] * 9,
        out_specs=[pl.BlockSpec(memory_space=pl.ANY)] * 2,
        scratch_shapes=scratch,
        compiler_params=pltpu.CompilerParams(
            collective_id=0, has_side_effects=True, vmem_limit_bytes=40 * 2**20
        ),
        name="physics_step",
    )(nodes, crm_state, cloud_mask, span_of.T, *consts)
    return dyn.reshape(4, 16, 8, LEV).transpose(0, 3, 1, 2), crm


def solution(mesh):
    return jax.shard_map(
        per_device,
        mesh=mesh,
        in_specs=(
            P(None, None, "blk", "row"),
            P(None, None, ("blk", "row")),
            P(None, ("blk", "row")),
            P(("blk", "row"), None),
        ),
        out_specs=(P(None, None, "blk", "row"), P(None, None, ("blk", "row"))),
        check_vma=False,
    )
```

```python
import functools

import jax
import jax.numpy as jnp
import numpy as np
from jax import lax
from jax.experimental import pallas as pl
from jax.experimental.pallas import tpu as pltpu
from jax.sharding import PartitionSpec as P

MESH = pl.DeviceIdType.MESH
LEV, CRM_LEV, CRM_COLS = 72, 58, 32
F32, BF16 = jnp.float32, jnp.bfloat16
SLOTS = ((0, -1), (0, 1), (-1, 0), (1, 0), (-1, -1), (-1, 1), (1, -1), (1, 1))
STATE_ROWS = (32, 32, 16, 16, 8, 8, 8, 8)
TILES, GROUPS = 4, 4
CELL_RANK = (16, 16, 8, 8, 2, 2, 2, 2)
CELL_ROWS = (24, 24, 16, 16, 8, 8, 8, 8)
STATE_AT = tuple(int(v) for v in np.cumsum((0,) + STATE_ROWS))
CELL_AT = tuple(int(v) for v in np.cumsum((0,) + CELL_ROWS))
HALO = CELL_AT[-1]


def poly_times(first_poly, second_poly):
    product = [0.0] * (len(first_poly) + len(second_poly) - 1)
    for i, first in enumerate(first_poly):
        for j, second in enumerate(second_poly):
            product[i + j] += first * second
    return product


def poly_slope(coeffs, point):
    return sum(power * coeffs[power] * point ** (power - 1) for power in range(1, len(coeffs)))


def poly_integral(coeffs, low, high):
    return sum(
        coeffs[power] * (high ** (power + 1) - low ** (power + 1)) / (power + 1)
        for power in range(len(coeffs))
    )


def element_tables():
    root_five = float(np.sqrt(5.0))
    gll_nodes = [-1.0, -1.0 / root_five, 1.0 / root_five, 1.0]
    weights = np.array([1.0 / 6.0, 5.0 / 6.0, 5.0 / 6.0, 1.0 / 6.0])
    derivative = np.zeros((4, 4))
    to_cells = np.zeros((2, 4))
    for basis in range(4):
        coeffs = [1.0]
        for other in range(4):
            if other != basis:
                denominator = gll_nodes[basis] - gll_nodes[other]
                coeffs = poly_times(coeffs, [-gll_nodes[other] / denominator, 1.0 / denominator])
        for node in range(4):
            derivative[node, basis] = poly_slope(coeffs, gll_nodes[node])
        to_cells[0, basis] = poly_integral(coeffs, -1.0, 0.0)
        to_cells[1, basis] = poly_integral(coeffs, 0.0, 1.0)
    to_nodes = np.array([[1.0, 0.0], [1.0, 0.0], [0.0, 1.0], [0.0, 1.0]])
    edge_weights = np.array([1.0 / 3.0, 5.0 / 6.0, 5.0 / 6.0, 1.0 / 3.0])
    return derivative, weights, to_cells, to_nodes, edge_weights


def line_operators(elements):
    derivative, weights, _, _, edge_weights = element_tables()
    count = elements * 4 * 3
    weight = np.tile(weights, elements * 3)
    fold = np.eye(count)
    for node in range(count):
        if node % 4 == 0:
            fold[node, (node - 1) % count] += 1.0
        if node % 4 == 3:
            fold[node, (node + 1) % count] += 1.0
    fold = fold / np.tile(edge_weights, elements * 3)[:, None]
    smooth = fold * weight
    stiff = np.kron(np.eye(elements * 3), derivative.T @ np.diag(weights) @ derivative)
    mine = slice(elements * 4, elements * 8)
    return smooth[mine], (fold @ stiff @ smooth)[mine], (smooth @ smooth)[mine]


def split(value):
    high = np.asarray(value, np.float32).astype(jnp.bfloat16)
    return high, (np.asarray(value, np.float32) - high.astype(np.float32)).astype(jnp.bfloat16)


@functools.cache
def tables():
    _, _, to_cells, to_nodes, _ = element_tables()
    smooth_x, stiff_x, mass_x = line_operators(4)
    smooth_y, stiff_y, mass_y = line_operators(2)
    nodes = np.kron(np.kron(np.eye(4), to_nodes), np.kron(np.eye(2), to_nodes))

    def block(dx, dy):
        x, y = slice(16 * (dx + 1), 16 * (dx + 2)), slice(8 * (dy + 1), 8 * (dy + 2))
        return np.kron(smooth_x[:, x], smooth_y[:, y]) - 0.01 * (
            np.kron(stiff_x[:, x], mass_y[:, y]) + np.kron(mass_x[:, x], stiff_y[:, y])
        )

    cell_sums = np.zeros((32, 128))
    cell_sums[:] = np.kron(np.kron(np.eye(4), to_cells), np.kron(np.eye(2), to_cells))
    mine = block(0, 0)
    own = np.zeros((128, 128))
    own[:, :32] = mine @ nodes
    outer, inner = np.zeros((128, 128)), np.zeros((128, 128))
    arrive = np.zeros((3, 128, 256))
    leave = np.zeros((2, HALO, 128))
    pick = np.zeros((HALO, 256), np.float32)
    for slot, (dx, dy) in enumerate(SLOTS):
        part = block(dx, dy)
        left, scale, right = np.linalg.svd(part)
        rank = int((scale > 1e-10).sum())
        assert rank <= STATE_ROWS[slot]
        at = STATE_AT[slot]
        outer[:, at : at + rank] = left[:, :rank] * np.sqrt(scale[:rank])
        inner[at : at + rank] = right[:rank] * np.sqrt(scale[:rank])[:, None]
        left, scale, right = np.linalg.svd(part @ nodes, full_matrices=False)
        rank = int((scale > 1e-10).sum())
        assert rank <= CELL_RANK[slot]
        left, right = left * np.sqrt(scale), right * np.sqrt(scale)[:, None]
        half = CELL_RANK[slot] // 2
        for field in range(3):
            at = CELL_AT[slot] + field * half
            pick[at : at + half, field::4] = 1.0
            for h in range(2):
                leave[h, at : at + half, :32] = right[h : 2 * half : 2]
                arrive[field, :, h * HALO + at : h * HALO + at + half] = left[:, h : 2 * half : 2]
    pieces = []
    for matrix in (cell_sums, inner, mine, outer, own, leave[0], leave[1]):
        pieces.extend(split(matrix))
    matrices = np.concatenate(pieces, axis=0)
    arrive = np.concatenate(split(arrive.reshape(384, 256)), axis=0)

    cell = np.arange(128)
    same = (cell[:, None] // 32) == (cell[None, :] // 32)
    step = (cell[:, None] - cell[None, :]) % 32
    east, west = same & (step == 1), same & (step == 31)
    along = np.concatenate([1.0 * east + 1.0 * west - same / 16.0, 1.0 * east - 1.0 * west], axis=1)
    along = np.concatenate([along, along], axis=0).astype(jnp.bfloat16)

    spread = np.zeros((16, 384))
    for s in range(2):
        for pair in range(2):
            for field in range(3):
                at = field * 128 + pair * 64 + s * 32
                spread[s * 8 + pair * 4 + field, at : at + 32] = 1.0
    means = (spread / 32.0).astype(jnp.bfloat16)
    wide = np.zeros((2, 2, TILES, 8, TILES, 384))
    for tile in range(TILES):
        wide[:, :, tile, :, tile] = spread.reshape(1, 2, 8, 384)
    spread = wide.reshape(32 * TILES, 384 * TILES).astype(jnp.bfloat16)
    return matrices, along, spread, means, pick, arrive


def halves(value):
    high = value.astype(BF16)
    return high, (value - high.astype(F32)).astype(BF16)


def dot(left, right):
    return jnp.dot(left, right, preferred_element_type=F32)


def dot_split(left, right):
    high, low = halves(right)
    return dot(left[0], high) + dot(left[1], high) + dot(left[0], low)


def iota(shape, axis):
    return lax.broadcasted_iota(jnp.int32, shape, axis)


def levels_moved(field, row):
    up = jnp.where(row == CRM_LEV - 1, field, pltpu.roll(field, 63, 0))
    down = jnp.where(row == 0, field, pltpu.roll(field, 1, 0))
    return up + down


def transported(field, along, momentum, row):
    return (
        0.4 * field
        + 0.15 * (along[:, :128] + levels_moved(field, row))
        + momentum * along[:, 128:]
    )


def condensed(heat, water, wet, saturation):
    cond = wet * jnp.maximum(water - 0.5 * heat - saturation, 0.0)
    return heat + 0.8 * cond, water - cond


def kernel(
    dyn, crm, mask, span, matrices, along_in, spread_in, means_in, pick_in, arrive_in,
    dyn_out, crm_out,
    xin, xb, mk, sp, mat, along, spread, means, pick, arrive,
    spans, xs, ys, wt, cat, og, ar, rs, rt, dh, dr, hs, hr, ob, od, place, post,
    load_sem, store_sem, go_sem, come_sem, tile_sem,
):
    p, r = lax.axis_index("blk"), lax.axis_index("row")
    rows, blocks = lax.axis_size("row"), lax.axis_size("blk")
    loads = [
        pltpu.make_async_copy(source, target, load_sem.at[k])
        for k, (source, target) in enumerate(
            ((span, sp), (dyn, xin), (matrices, mat), (crm, xb), (mask, mk), (along_in, along),
             (spread_in, spread), (means_in, means), (pick_in, pick), (arrive_in, arrive))
        )
    ]
    for load in loads:
        load.start()

    barrier = pltpu.get_barrier_semaphore()

    def greet(k, carry):
        pl.semaphore_signal(
            barrier, inc=1, device_id=(p, lax.rem(r + k, rows)), device_id_type=MESH
        )
        return carry

    lax.fori_loop(1, rows, greet, None)
    around = [
        (lax.rem(p + blocks - dx, blocks), lax.rem(r + rows - dy, rows)) for dx, dy in SLOTS
    ]
    for slot in range(2, 8):
        pl.semaphore_signal(barrier, inc=1, device_id=around[slot], device_id_type=MESH)

    cat[...] = jnp.zeros_like(cat)
    spans[...] = jnp.zeros_like(spans)

    def table(k, lines=128):
        at = (0, 64, 320, 576, 832, 1088, 1088 + 2 * HALO)[k]
        return mat[at : at + lines], mat[at + lines : at + 2 * lines]

    loads[0].wait()
    spans[0:1, 0:32] = sp[...].astype(F32)
    named = spans[...]
    named = named + pltpu.roll(named, 32, 1)
    named = named + pltpu.roll(named, 64, 1)
    lane, line = iota((32, 128), 1), iota((32, 128), 0)
    across = jnp.broadcast_to(named[0:1, :], (32, 128))
    down = jnp.sum(jnp.where(lane == line, across, 0.0), axis=1, keepdims=True)
    earlier = jnp.where((down == across) & (line < (lane & 31)), 1.0, 0.0)
    position = 2.0 * named[0:1, :] + jnp.sum(earlier, axis=0, keepdims=True)
    lane, line = iota((128, 128), 1), iota((128, 128), 0)
    wanted = (2 * line - (line & 3)).astype(F32)
    offered = 4.0 * jnp.broadcast_to(position, (128, 128)) + (lane >> 5).astype(F32)
    send_to = jnp.concatenate(
        [jnp.where(offered - 4.0 * s == wanted, 1.0, 0.0) for s in range(2)], axis=1
    ).astype(BF16)

    loads[1].wait()
    loads[2].wait()
    for field in range(3):
        cat[32 * field : 32 * field + 32, 0:LEV] = dot_split(table(0, 32), xin[field])
    first = jnp.where(lane < CRM_LEV, cat[...], 0.0)
    high, low = halves(jnp.concatenate([first, pltpu.roll(first, 64, 1)], axis=0))
    sent = dot(send_to, jnp.concatenate([high, low], axis=1))
    og[...] = (sent[:, :128] + sent[:, 128:]).reshape(32, 4, 128)

    pl.semaphore_wait(barrier, rows - 1 + 6)

    def profile_copy(target):
        return pltpu.make_async_remote_copy(
            src_ref=og.at[target], dst_ref=ar.at[r], send_sem=go_sem.at[0],
            recv_sem=tile_sem.at[lax.div(r, 2 * TILES)], device_id=(p, target), device_id_type=MESH,
        )

    def send_profile(k, carry):
        away = 16 + (1 - 2 * (k & 1)) * ((k + 1) >> 1)
        profile_copy(lax.rem(r + away, rows)).start()
        return carry

    lax.fori_loop(0, rows - 1, send_profile, None)
    ar[r] = og[r]

    def clear(j, carry):
        for field in range(3):
            xs[j, 64 * field + 56 : 64 * field + 64, :] = jnp.zeros((8, 128), F32)
        wt[j, 56:64, :] = jnp.zeros((8, 128), F32)
        return carry

    lax.fori_loop(0, 16, clear, None, unroll=4)

    for field in range(4):
        dh[:, 128 * field : 128 * field + LEV] = dot_split(table(1), xin[field])
    state_copies = []
    for slot in range(8):
        at = pl.ds(STATE_AT[slot], STATE_ROWS[slot])
        state_copies.append(
            pltpu.make_async_remote_copy(
                src_ref=dh.at[at], dst_ref=dr.at[at], send_sem=go_sem.at[1],
                recv_sem=come_sem.at[1], device_id=around[slot], device_id_type=MESH,
            )
        )
        state_copies[-1].start()

    for k in range(3, 6):
        loads[k].wait()
    row = iota((64, 128), 0)
    saturation = 0.5 - row.astype(F32) / CRM_LEV

    def begin(j, carry):
        at = pl.ds(pl.multiple_of(j * 128, 128), 128)
        for field in range(3):
            xs[j, 64 * field : 64 * field + CRM_LEV, :] = xb[field, :, at].astype(F32)
        wt[j, 0:CRM_LEV, :] = 0.5 * mk[:, at].astype(F32)
        state = xs[j]
        shifted = dot(state.astype(BF16), along[0:128, :])
        momentum = -0.1 * state[128:192]
        for field in range(3):
            part = slice(64 * field, 64 * field + 64)
            ys[j, part, :] = transported(state[part], shifted[part], momentum, row)
        return carry

    lax.fori_loop(0, 16, begin, None, unroll=2)

    for field in range(4):
        od[field] = dot_split(table(2), xin[field])

    for k in range(6, 10):
        loads[k].wait()
    lane, line = iota((32, 128), 1), iota((32, 128), 0)
    home = jnp.sum(
        jnp.where(lane == line, jnp.broadcast_to(position, (32, 128)), 0.0), axis=1, keepdims=True
    )
    code = (lane >> 2).astype(F32)
    match = jnp.concatenate(
        [jnp.where(home - s == 2.0 * code, 1.0, 0.0) for s in range(2)], axis=1
    )
    lane = iota((32, 256), 1)
    for field in range(3):
        place[32 * field : 32 * field + 32, :] = jnp.where((lane & 3) == field, match, 0.0).astype(BF16)
    match = match.astype(BF16)
    for h in range(2):
        for half, piece in enumerate(table(5 + h, HALO)):
            post[half * HALO : (half + 1) * HALO, 256 * h : 256 * h + 256] = (
                pick[...] * dot(piece[:, 0:32], match)
            ).astype(BF16)

    def all_of(source, target, k):
        return pltpu.make_async_remote_copy(
            src_ref=source.at[pl.ds(0, 31)], dst_ref=target.at[pl.ds(0, 31)],
            send_sem=go_sem.at[k], recv_sem=come_sem.at[k],
            device_id=(p, lax.rem(r + 1, rows)), device_id_type=MESH,
        )

    def tendency_copy(target):
        return pltpu.make_async_remote_copy(
            src_ref=rs.at[target], dst_ref=rt.at[r], send_sem=go_sem.at[2],
            recv_sem=come_sem.at[2], device_id=(p, target), device_id_type=MESH,
        )

    mine = lax.div(r, 2 * TILES)

    def finish(group, own):
        first = pl.multiple_of(group * TILES, TILES)
        near = ar.at[pl.ds(2 * first, 2 * TILES)]
        due = ar.at[pl.ds(2 * first, 2 * TILES - own)]
        pltpu.make_async_copy(due, due, tile_sem.at[group]).wait()
        near = near[...].reshape(8 * TILES, 128)
        near = jnp.concatenate([near, pltpu.roll(near, 64, 1)], axis=0)
        high, low = halves(near)
        near = jnp.concatenate([high.astype(F32), low.astype(F32)], axis=0).T[0:64]
        pulled = 0.3 * dot(near.astype(BF16), spread[...])
        pulled = [
            [pulled[:, 128 * (3 * t + f) : 128 * (3 * t + f + 1)] for f in range(3)]
            for t in range(TILES)
        ]
        fields = []
        for t in range(TILES):
            one = [ys[first + t, 64 * f : 64 * f + 64, :] + pulled[t][f] for f in range(3)]
            one[0], one[1] = condensed(one[0], one[1], wt[first + t], saturation)
            fields.append(one)
        both = [jnp.concatenate(halves(value), axis=1) for one in fields for value in one]
        shifted = dot(jnp.concatenate(both, axis=0), along[...])
        change = []
        for t in range(TILES):
            at = pl.ds(pl.multiple_of(128 * (first + t), 128), 128)
            one = fields[t]
            momentum = -0.1 * one[2]
            two = []
            for f in range(3):
                line = 64 * (3 * t + f)
                moved = transported(one[f], shifted[line : line + 64], momentum, row)
                two.append(moved + pulled[t][f])
            two[0], two[1] = condensed(two[0], two[1], wt[first + t], saturation)
            parts = []
            for f in range(3):
                ob[f, :, at] = two[f][0:CRM_LEV].astype(BF16)
                parts.append(halves(two[f] - xs[first + t, 64 * f : 64 * f + 64, :]))
            change += [jnp.concatenate([part[h] for part in parts], axis=1) for h in range(2)]
        mean = lax.dot_general(
            means[...], jnp.concatenate(change, axis=0), (((1,), (1,)), ((), ())),
            preferred_element_type=F32,
        )
        for t in range(TILES):
            part = mean[:, 128 * t : 128 * t + 128]
            part = part + pltpu.roll(part, 64, 1)
            message = jnp.where(iota((8, 128), 1) < 64, part[0:8], part[8:16])
            for pair in range(2):
                rs[2 * (first + t) + pair] = message[4 * pair : 4 * pair + 4]
        for k in range(2 * TILES):
            target = 2 * first + k
            if own:
                pl.when(target != r)(tendency_copy(target).start)
            else:
                tendency_copy(target).start()

    def others(k, carry):
        away = GROUPS // 2 + (1 - 2 * (k & 1)) * ((k + 1) >> 1)
        finish(lax.rem(mine + away, GROUPS), 0)
        return carry

    lax.fori_loop(0, GROUPS - 1, others, None)
    finish(mine, 1)
    rt[r] = rs[r]

    store = pltpu.make_async_copy(ob, crm_out, store_sem.at[0])
    store.start()

    pltpu.make_async_remote_copy(
        src_ref=dh, dst_ref=dr, send_sem=go_sem.at[1], recv_sem=come_sem.at[1],
        device_id=around[0], device_id_type=MESH,
    ).wait_recv()
    for field in range(4):
        od[field] += dot_split(table(3), dr[:, 128 * field : 128 * field + 128])[:, 0:LEV]

    all_of(rs, rt, 2).wait_recv()
    given = rt[...].reshape(128, 128)
    lane = iota((128, 128), 1)
    given = [jnp.where(lane < CRM_LEV, value, 0.0) for value in (given, pltpu.roll(given, 64, 1))]
    given = jnp.concatenate(halves(jnp.concatenate(given, axis=0)), axis=1)
    turned = jnp.concatenate(
        [pltpu.roll(given[:, 128 * k : 128 * k + 128].astype(F32), 64, 1) for k in range(2)], axis=1
    ).astype(BF16)
    sent = dot(post[...], jnp.concatenate([given, turned], axis=0))
    hs[...] = sent[0:HALO, 0:128] + sent[0:HALO, 128:256] + sent[HALO:, 0:128]
    cell_copies = []
    for slot in range(8):
        at = pl.ds(CELL_AT[slot], CELL_ROWS[slot])
        cell_copies.append(
            pltpu.make_async_remote_copy(
                src_ref=hs.at[at], dst_ref=hr.at[at], send_sem=go_sem.at[3],
                recv_sem=come_sem.at[3], device_id=around[slot], device_id_type=MESH,
            )
        )
        cell_copies[-1].start()
    cells = dot(place[...], given)
    cells = cells[:, 0:128] + cells[:, 128:256]
    own = table(4)
    own = own[0][:, 0:32], own[1][:, 0:32]
    for field in range(3):
        od[field] += dot_split(own, cells[32 * field : 32 * field + 32])[:, 0:LEV]

    halo_copy = pltpu.make_async_remote_copy(
        src_ref=hs, dst_ref=hr, send_sem=go_sem.at[3],
        recv_sem=come_sem.at[3], device_id=around[0], device_id_type=MESH,
    )
    halo_copy.wait_recv()
    lane = iota((HALO, 128), 1)
    came = hr[...]
    came = [jnp.where(lane < 64, value, 0.0) for value in (came, pltpu.roll(came, 64, 1))]
    came = jnp.concatenate(came + [jnp.zeros((256 - 2 * HALO, 128), F32)], axis=0)
    came = jnp.concatenate(halves(came), axis=1)
    for field in range(3):
        high = dot(arrive[128 * field : 128 * field + 128, :], came)
        low = dot(arrive[384 + 128 * field : 512 + 128 * field, :], came[:, 0:128])
        od[field] += (high[:, 0:128] + high[:, 128:256] + low)[:, 0:LEV]
    final = pltpu.make_async_copy(od, dyn_out, store_sem.at[1])
    final.start()
    all_of(og, ar, 0).wait_send()
    all_of(rs, rt, 2).wait_send()
    pltpu.make_async_remote_copy(
        src_ref=dh, dst_ref=dr, send_sem=go_sem.at[1], recv_sem=come_sem.at[1],
        device_id=around[0], device_id_type=MESH,
    ).wait_send()
    halo_copy.wait_send()
    store.wait()
    final.wait()


def per_device(dyn_state, crm_state, cloud_mask, span_of):
    consts = tuple(jnp.asarray(value) for value in tables())
    vmem = pltpu.VMEM
    scratch = [
        vmem((4, 128, LEV), F32), vmem((3, CRM_LEV, 2048), BF16), vmem((CRM_LEV, 2048), jnp.int32),
        vmem((1, 32), jnp.int32),
    ]
    scratch += [vmem(value.shape, value.dtype) for value in consts]
    scratch += [
        vmem((8, 128), F32),
        vmem((16, 192, 128), F32), vmem((16, 192, 128), F32), vmem((16, 64, 128), F32),
        vmem((128, 128), F32),
        vmem((32, 4, 128), F32), vmem((32, 4, 128), F32),
        vmem((32, 4, 128), F32), vmem((32, 4, 128), F32),
        vmem((128, 512), F32), vmem((128, 512), F32),
        vmem((HALO, 128), F32), vmem((HALO, 128), F32),
        vmem((3, CRM_LEV, 2048), BF16), vmem((4, 128, LEV), F32),
        vmem((96, 256), BF16), vmem((2 * HALO, 512), BF16),
        pltpu.SemaphoreType.DMA((10,)), pltpu.SemaphoreType.DMA((2,)),
        pltpu.SemaphoreType.DMA((4,)), pltpu.SemaphoreType.DMA((4,)), pltpu.SemaphoreType.DMA((GROUPS,)),
    ]
    nodes = dyn_state.transpose(0, 2, 3, 1).reshape(4, 128, LEV)
    operands = (nodes, crm_state, cloud_mask, span_of.T, *consts)
    dyn, crm = pl.pallas_call(
        kernel,
        out_shape=(
            jax.ShapeDtypeStruct((4, 128, LEV), F32),
            jax.ShapeDtypeStruct((3, CRM_LEV, 2048), BF16),
        ),
        in_specs=[pl.BlockSpec(memory_space=pl.ANY)] * 10,
        out_specs=[pl.BlockSpec(memory_space=pl.ANY)] * 2,
        scratch_shapes=scratch,
        compiler_params=pltpu.CompilerParams(
            collective_id=0, has_side_effects=True, vmem_limit_bytes=40 * 2**20
        ),
        name="physics_step",
    )(*(pltpu.with_memory_space_constraint(value, pltpu.HBM) for value in operands))
    return dyn.reshape(4, 16, 8, LEV).transpose(0, 3, 1, 2), crm


def solution(mesh):
    return jax.shard_map(
        per_device,
        mesh=mesh,
        in_specs=(
            P(None, None, "blk", "row"),
            P(None, None, ("blk", "row")),
            P(None, ("blk", "row")),
            P(("blk", "row"), None),
        ),
        out_specs=(P(None, None, "blk", "row"), P(None, None, ("blk", "row"))),
        check_vma=False,
    )
```

```python
import functools

import jax
import jax.numpy as jnp
import numpy as np
from jax import lax
from jax.experimental import pallas as pl
from jax.experimental.pallas import tpu as pltpu
from jax.sharding import PartitionSpec as P

MESH = pl.DeviceIdType.MESH
LEV, CRM_LEV, CRM_COLS = 72, 58, 32
F32, BF16 = jnp.float32, jnp.bfloat16
SLOTS = ((0, -1), (0, 1), (-1, 0), (1, 0), (-1, -1), (-1, 1), (1, -1), (1, 1))
STATE_ROWS = (32, 32, 16, 16, 8, 8, 8, 8)
TILES, GROUPS = 4, 4
CELL_RANK = (16, 16, 8, 8, 2, 2, 2, 2)
CELL_ROWS = (24, 24, 16, 16, 8, 8, 8, 8)
STATE_AT = tuple(int(v) for v in np.cumsum((0,) + STATE_ROWS))
CELL_AT = tuple(int(v) for v in np.cumsum((0,) + CELL_ROWS))
HALO = CELL_AT[-1]


def poly_times(first_poly, second_poly):
    product = [0.0] * (len(first_poly) + len(second_poly) - 1)
    for i, first in enumerate(first_poly):
        for j, second in enumerate(second_poly):
            product[i + j] += first * second
    return product


def poly_slope(coeffs, point):
    return sum(power * coeffs[power] * point ** (power - 1) for power in range(1, len(coeffs)))


def poly_integral(coeffs, low, high):
    return sum(
        coeffs[power] * (high ** (power + 1) - low ** (power + 1)) / (power + 1)
        for power in range(len(coeffs))
    )


def element_tables():
    root_five = float(np.sqrt(5.0))
    gll_nodes = [-1.0, -1.0 / root_five, 1.0 / root_five, 1.0]
    weights = np.array([1.0 / 6.0, 5.0 / 6.0, 5.0 / 6.0, 1.0 / 6.0])
    derivative = np.zeros((4, 4))
    to_cells = np.zeros((2, 4))
    for basis in range(4):
        coeffs = [1.0]
        for other in range(4):
            if other != basis:
                denominator = gll_nodes[basis] - gll_nodes[other]
                coeffs = poly_times(coeffs, [-gll_nodes[other] / denominator, 1.0 / denominator])
        for node in range(4):
            derivative[node, basis] = poly_slope(coeffs, gll_nodes[node])
        to_cells[0, basis] = poly_integral(coeffs, -1.0, 0.0)
        to_cells[1, basis] = poly_integral(coeffs, 0.0, 1.0)
    to_nodes = np.array([[1.0, 0.0], [1.0, 0.0], [0.0, 1.0], [0.0, 1.0]])
    edge_weights = np.array([1.0 / 3.0, 5.0 / 6.0, 5.0 / 6.0, 1.0 / 3.0])
    return derivative, weights, to_cells, to_nodes, edge_weights


def line_operators(elements):
    derivative, weights, _, _, edge_weights = element_tables()
    count = elements * 4 * 3
    weight = np.tile(weights, elements * 3)
    fold = np.eye(count)
    for node in range(count):
        if node % 4 == 0:
            fold[node, (node - 1) % count] += 1.0
        if node % 4 == 3:
            fold[node, (node + 1) % count] += 1.0
    fold = fold / np.tile(edge_weights, elements * 3)[:, None]
    smooth = fold * weight
    stiff = np.kron(np.eye(elements * 3), derivative.T @ np.diag(weights) @ derivative)
    mine = slice(elements * 4, elements * 8)
    return smooth[mine], (fold @ stiff @ smooth)[mine], (smooth @ smooth)[mine]


def split(value):
    high = np.asarray(value, np.float32).astype(jnp.bfloat16)
    return high, (np.asarray(value, np.float32) - high.astype(np.float32)).astype(jnp.bfloat16)


@functools.cache
def tables():
    _, _, to_cells, to_nodes, _ = element_tables()
    smooth_x, stiff_x, mass_x = line_operators(4)
    smooth_y, stiff_y, mass_y = line_operators(2)
    nodes = np.kron(np.kron(np.eye(4), to_nodes), np.kron(np.eye(2), to_nodes))

    def block(dx, dy):
        x, y = slice(16 * (dx + 1), 16 * (dx + 2)), slice(8 * (dy + 1), 8 * (dy + 2))
        return np.kron(smooth_x[:, x], smooth_y[:, y]) - 0.01 * (
            np.kron(stiff_x[:, x], mass_y[:, y]) + np.kron(mass_x[:, x], stiff_y[:, y])
        )

    cell_sums = np.zeros((32, 128))
    cell_sums[:] = np.kron(np.kron(np.eye(4), to_cells), np.kron(np.eye(2), to_cells))
    mine = block(0, 0)
    own = np.zeros((128, 128))
    own[:, :32] = mine @ nodes
    outer, inner = np.zeros((128, 128)), np.zeros((128, 128))
    arrive = np.zeros((3, 128, 256))
    leave = np.zeros((2, HALO, 128))
    pick = np.zeros((HALO, 256), np.float32)
    for slot, (dx, dy) in enumerate(SLOTS):
        part = block(dx, dy)
        left, scale, right = np.linalg.svd(part)
        rank = int((scale > 1e-10).sum())
        assert rank <= STATE_ROWS[slot]
        at = STATE_AT[slot]
        outer[:, at : at + rank] = left[:, :rank] * np.sqrt(scale[:rank])
        inner[at : at + rank] = right[:rank] * np.sqrt(scale[:rank])[:, None]
        left, scale, right = np.linalg.svd(part @ nodes, full_matrices=False)
        rank = int((scale > 1e-10).sum())
        assert rank <= CELL_RANK[slot]
        left, right = left * np.sqrt(scale), right * np.sqrt(scale)[:, None]
        half = CELL_RANK[slot] // 2
        for field in range(3):
            at = CELL_AT[slot] + field * half
            pick[at : at + half, field::4] = 1.0
            for h in range(2):
                leave[h, at : at + half, :32] = right[h : 2 * half : 2]
                arrive[field, :, h * HALO + at : h * HALO + at + half] = left[:, h : 2 * half : 2]
    pieces = []
    for matrix in (inner, mine, outer, own, leave[0], leave[1]):
        pieces.extend(split(matrix))
    matrices = np.concatenate(pieces, axis=0)
    cell_sums = np.concatenate(split(cell_sums), axis=0)
    arrive = np.concatenate(split(arrive.reshape(384, 256)), axis=0)

    cell = np.arange(128)
    same = (cell[:, None] // 32) == (cell[None, :] // 32)
    step = (cell[:, None] - cell[None, :]) % 32
    east, west = same & (step == 1), same & (step == 31)
    along = np.concatenate([1.0 * east + 1.0 * west - same / 16.0, 1.0 * east - 1.0 * west], axis=1)
    along = np.concatenate([along, along], axis=0).astype(jnp.bfloat16)

    spread = np.zeros((16, 384))
    for s in range(2):
        for pair in range(2):
            for field in range(3):
                at = field * 128 + pair * 64 + s * 32
                spread[s * 8 + pair * 4 + field, at : at + 32] = 1.0
    means = (spread / 32.0).astype(jnp.bfloat16)
    wide = np.zeros((2, 2, TILES, 8, TILES, 384))
    for tile in range(TILES):
        wide[:, :, tile, :, tile] = spread.reshape(1, 2, 8, 384)
    spread = wide.reshape(32 * TILES, 384 * TILES).astype(jnp.bfloat16)
    return cell_sums, matrices, along, spread, means, pick, arrive


def halves(value):
    high = value.astype(BF16)
    return high, (value - high.astype(F32)).astype(BF16)


def dot(left, right):
    return jnp.dot(left, right, preferred_element_type=F32)


def dot_split(left, right):
    high, low = halves(right)
    return dot(left[0], high) + dot(left[1], high) + dot(left[0], low)


def iota(shape, axis):
    return lax.broadcasted_iota(jnp.int32, shape, axis)


def levels_moved(field, row):
    up = jnp.where(row == CRM_LEV - 1, field, pltpu.roll(field, 63, 0))
    down = jnp.where(row == 0, field, pltpu.roll(field, 1, 0))
    return up + down


def transported(field, along, momentum, row):
    return (
        0.4 * field
        + 0.15 * (along[:, :128] + levels_moved(field, row))
        + momentum * along[:, 128:]
    )


def condensed(heat, water, wet, saturation):
    cond = wet * jnp.maximum(water - 0.5 * heat - saturation, 0.0)
    return heat + 0.8 * cond, water - cond


def kernel(
    dyn, crm, mask, span, sums_in, matrices, along_in, spread_in, means_in, pick_in,
    hr, part_out, crm_out,
    xin, xb, mk, sp, sums, mat, along, spread, means, pick,
    spans, xs, ys, wt, cat, og, ar, rs, rt, dh, dr, hs, ob, od, place, post,
    load_sem, store_sem, go_sem, come_sem, tile_sem,
):
    p, r = lax.axis_index("blk"), lax.axis_index("row")
    rows, blocks = lax.axis_size("row"), lax.axis_size("blk")
    barrier = pltpu.get_barrier_semaphore()

    def far_first(k):
        return lax.rem(r + 16 + (1 - 2 * (k & 1)) * ((k + 1) >> 1), rows)

    def greet(k, carry):
        pl.semaphore_signal(barrier, inc=1, device_id=(p, far_first(k)), device_id_type=MESH)
        return carry

    lax.fori_loop(0, rows - 1, greet, None)
    around = [
        (lax.rem(p + blocks - dx, blocks), lax.rem(r + rows - dy, rows)) for dx, dy in SLOTS
    ]
    for slot in range(2, 8):
        pl.semaphore_signal(barrier, inc=1, device_id=around[slot], device_id_type=MESH)

    loads = [
        pltpu.make_async_copy(source, target, load_sem.at[k])
        for k, (source, target) in enumerate(
            ((span, sp), (sums_in, sums), (dyn, xin), (crm, xb), (mask, mk), (along_in, along),
             (spread_in, spread), (means_in, means), (matrices, mat), (pick_in, pick))
        )
    ]
    for load in loads[:3]:
        load.start()

    cat[...] = jnp.zeros_like(cat)
    spans[...] = jnp.zeros_like(spans)

    def table(k, lines=128):
        at = (0, 256, 512, 768, 1024, 1024 + 2 * HALO)[k]
        return mat[at : at + lines], mat[at + lines : at + 2 * lines]

    loads[0].wait()
    spans[0:1, 0:32] = sp[...].astype(F32)
    named = spans[...]
    named = named + pltpu.roll(named, 32, 1)
    named = named + pltpu.roll(named, 64, 1)
    lane, line = iota((32, 128), 1), iota((32, 128), 0)
    across = jnp.broadcast_to(named[0:1, :], (32, 128))
    down = jnp.sum(jnp.where(lane == line, across, 0.0), axis=1, keepdims=True)
    earlier = jnp.where((down == across) & (line < (lane & 31)), 1.0, 0.0)
    position = 2.0 * named[0:1, :] + jnp.sum(earlier, axis=0, keepdims=True)
    lane, line = iota((128, 128), 1), iota((128, 128), 0)
    wanted = (2 * line - (line & 3)).astype(F32)
    offered = 4.0 * jnp.broadcast_to(position, (128, 128)) + (lane >> 5).astype(F32)
    send_to = jnp.concatenate(
        [jnp.where(offered - 4.0 * s == wanted, 1.0, 0.0) for s in range(2)], axis=1
    ).astype(BF16)

    loads[1].wait()
    loads[2].wait()
    for load in loads[3:6]:
        load.start()
    for field in range(3):
        cat[32 * field : 32 * field + 32, 0:LEV] = dot_split((sums[0:32], sums[32:64]), xin[field])
    first = jnp.where(lane < CRM_LEV, cat[...], 0.0)
    high, low = halves(jnp.concatenate([first, pltpu.roll(first, 64, 1)], axis=0))
    sent = dot(send_to, jnp.concatenate([high, low], axis=1))
    og[...] = (sent[:, :128] + sent[:, 128:]).reshape(32, 4, 128)

    pl.semaphore_wait(barrier, rows - 1 + 6)

    def profile_copy(target):
        return pltpu.make_async_remote_copy(
            src_ref=og.at[target], dst_ref=ar.at[r], send_sem=go_sem.at[0],
            recv_sem=tile_sem.at[lax.div(r, 2 * TILES)], device_id=(p, target), device_id_type=MESH,
        )

    def send_profile(k, carry):
        away = (1 - 2 * (k & 1)) * ((k + 2) >> 1)
        profile_copy(lax.rem(r + rows + away, rows)).start()
        return carry

    lax.fori_loop(0, rows - 1, send_profile, None)
    ar[r] = og[r]

    for load in loads[6:]:
        load.start()

    for k in range(3, 6):
        loads[k].wait()
    row = iota((64, 128), 0)
    saturation = 0.5 - row.astype(F32) / CRM_LEV
    rest = jnp.zeros((64 - CRM_LEV, 128), F32)

    def begin(group, carry):
        first = pl.multiple_of(group * TILES, TILES)
        state = []
        for t in range(TILES):
            at = pl.ds(pl.multiple_of(128 * (first + t), 128), 128)
            wt[first + t] = jnp.concatenate([0.5 * mk[:, at].astype(F32), rest], axis=0)
            for f in range(3):
                state.append(jnp.concatenate([xb[f, :, at].astype(F32), rest], axis=0))
                xs[first + t, 64 * f : 64 * f + 64, :] = state[-1]
        shifted = dot(jnp.concatenate(state, axis=0).astype(BF16), along[0:128, :])
        for t in range(TILES):
            momentum = -0.1 * state[3 * t + 2]
            for f in range(3):
                line = 64 * (3 * t + f)
                moved = transported(state[3 * t + f], shifted[line : line + 64], momentum, row)
                ys[first + t, 64 * f : 64 * f + 64, :] = moved
        return carry

    lax.fori_loop(0, GROUPS, begin, None)
    loads[6].wait()
    loads[7].wait()

    def all_of(source, target, k):
        return pltpu.make_async_remote_copy(
            src_ref=source.at[pl.ds(0, 31)], dst_ref=target.at[pl.ds(0, 31)],
            send_sem=go_sem.at[k], recv_sem=come_sem.at[k],
            device_id=(p, lax.rem(r + 1, rows)), device_id_type=MESH,
        )

    def tendency_copy(target):
        return pltpu.make_async_remote_copy(
            src_ref=rs.at[target], dst_ref=rt.at[r], send_sem=go_sem.at[2],
            recv_sem=come_sem.at[2], device_id=(p, target), device_id_type=MESH,
        )

    mine = lax.div(r, 2 * TILES)

    def finish(group, own):
        first = pl.multiple_of(group * TILES, TILES)
        near = ar.at[pl.ds(2 * first, 2 * TILES)]
        due = ar.at[pl.ds(2 * first, 2 * TILES - own)]
        pltpu.make_async_copy(due, due, tile_sem.at[group]).wait()
        near = near[...].reshape(8 * TILES, 128)
        near = jnp.concatenate([near, pltpu.roll(near, 64, 1)], axis=0)
        high, low = halves(near)
        near = jnp.concatenate([high.astype(F32), low.astype(F32)], axis=0).T[0:64]
        pulled = 0.3 * dot(near.astype(BF16), spread[...])
        pulled = [
            [pulled[:, 128 * (3 * t + f) : 128 * (3 * t + f + 1)] for f in range(3)]
            for t in range(TILES)
        ]
        fields = []
        for t in range(TILES):
            one = [ys[first + t, 64 * f : 64 * f + 64, :] + pulled[t][f] for f in range(3)]
            one[0], one[1] = condensed(one[0], one[1], wt[first + t], saturation)
            fields.append(one)
        both = [jnp.concatenate(halves(value), axis=1) for one in fields for value in one]
        shifted = dot(jnp.concatenate(both, axis=0), along[...])
        change = []
        for t in range(TILES):
            at = pl.ds(pl.multiple_of(128 * (first + t), 128), 128)
            one = fields[t]
            momentum = -0.1 * one[2]
            two = []
            for f in range(3):
                line = 64 * (3 * t + f)
                moved = transported(one[f], shifted[line : line + 64], momentum, row)
                two.append(moved + pulled[t][f])
            two[0], two[1] = condensed(two[0], two[1], wt[first + t], saturation)
            parts = []
            for f in range(3):
                ob[f, :, at] = two[f][0:CRM_LEV].astype(BF16)
                parts.append(halves(two[f] - xs[first + t, 64 * f : 64 * f + 64, :]))
            change += [jnp.concatenate([part[h] for part in parts], axis=1) for h in range(2)]
        mean = lax.dot_general(
            means[...], jnp.concatenate(change, axis=0), (((1,), (1,)), ((), ())),
            preferred_element_type=F32,
        )
        for t in range(TILES):
            part = mean[:, 128 * t : 128 * t + 128]
            part = part + pltpu.roll(part, 64, 1)
            message = jnp.where(iota((8, 128), 1) < 64, part[0:8], part[8:16])
            for pair in range(2):
                rs[2 * (first + t) + pair] = message[4 * pair : 4 * pair + 4]
        for k in range(2 * TILES):
            target = 2 * first + k
            if own:
                pl.when(target != r)(tendency_copy(target).start)
            else:
                tendency_copy(target).start()

    def others(k, carry):
        away = (1 - 2 * (k & 1)) * ((k + 2) >> 1)
        finish(lax.rem(mine + GROUPS + away, GROUPS), 0)
        return carry

    finish(mine, 1)
    lax.fori_loop(0, GROUPS - 1, others, None)
    rt[r] = rs[r]

    store = pltpu.make_async_copy(ob, crm_out, store_sem.at[0])
    store.start()

    loads[8].wait()
    for field in range(4):
        dh[:, 128 * field : 128 * field + LEV] = dot_split(table(0), xin[field])
    state_copies = []
    for slot in range(8):
        at = pl.ds(STATE_AT[slot], STATE_ROWS[slot])
        state_copies.append(
            pltpu.make_async_remote_copy(
                src_ref=dh.at[at], dst_ref=dr.at[at], send_sem=go_sem.at[1],
                recv_sem=come_sem.at[1], device_id=around[slot], device_id_type=MESH,
            )
        )
        state_copies[-1].start()

    loads[9].wait()
    lane, line = iota((32, 128), 1), iota((32, 128), 0)
    home = jnp.sum(
        jnp.where(lane == line, jnp.broadcast_to(position, (32, 128)), 0.0), axis=1, keepdims=True
    )
    code = (lane >> 2).astype(F32)
    match = jnp.concatenate(
        [jnp.where(home - s == 2.0 * code, 1.0, 0.0) for s in range(2)], axis=1
    )
    lane = iota((32, 256), 1)
    for field in range(3):
        place[32 * field : 32 * field + 32, :] = jnp.where((lane & 3) == field, match, 0.0).astype(BF16)
    match = match.astype(BF16)
    for h in range(2):
        for half, piece in enumerate(table(4 + h, HALO)):
            post[half * HALO : (half + 1) * HALO, 256 * h : 256 * h + 256] = (
                pick[...] * dot(piece[:, 0:32], match)
            ).astype(BF16)

    for field in range(4):
        od[field, :, 0:LEV] = dot_split(table(1), xin[field])

    all_of(rs, rt, 2).wait_recv()
    given = rt[...].reshape(128, 128)
    lane = iota((128, 128), 1)
    given = [jnp.where(lane < CRM_LEV, value, 0.0) for value in (given, pltpu.roll(given, 64, 1))]
    given = jnp.concatenate(halves(jnp.concatenate(given, axis=0)), axis=1)
    turned = jnp.concatenate(
        [pltpu.roll(given[:, 128 * k : 128 * k + 128].astype(F32), 64, 1) for k in range(2)], axis=1
    ).astype(BF16)
    sent = dot(post[...], jnp.concatenate([given, turned], axis=0))
    hs[...] = sent[0:HALO, 0:128] + sent[0:HALO, 128:256] + sent[HALO:, 0:128]
    cell_copies = []
    for slot in range(8):
        at = pl.ds(CELL_AT[slot], CELL_ROWS[slot])
        cell_copies.append(
            pltpu.make_async_remote_copy(
                src_ref=hs.at[at], dst_ref=hr.at[at], send_sem=go_sem.at[3],
                recv_sem=come_sem.at[3], device_id=around[slot], device_id_type=MESH,
            )
        )
        cell_copies[-1].start()
    cells = dot(place[...], given)
    cells = cells[:, 0:128] + cells[:, 128:256]
    own = table(3)
    own = own[0][:, 0:32], own[1][:, 0:32]
    for field in range(3):
        od[field, :, 0:LEV] += dot_split(own, cells[32 * field : 32 * field + 32])[:, 0:LEV]

    pltpu.make_async_remote_copy(
        src_ref=dh, dst_ref=dr, send_sem=go_sem.at[1], recv_sem=come_sem.at[1],
        device_id=around[0], device_id_type=MESH,
    ).wait_recv()
    for field in range(4):
        od[field, :, 0:LEV] += dot_split(table(2), dr[:, 128 * field : 128 * field + 128])[:, 0:LEV]

    halo_copy = pltpu.make_async_remote_copy(
        src_ref=hs, dst_ref=hr, send_sem=go_sem.at[3],
        recv_sem=come_sem.at[3], device_id=around[0], device_id_type=MESH,
    )
    part = pltpu.make_async_copy(od, part_out, store_sem.at[1])
    part.start()
    halo_copy.wait_recv()
    all_of(og, ar, 0).wait_send()
    all_of(rs, rt, 2).wait_send()
    pltpu.make_async_remote_copy(
        src_ref=dh, dst_ref=dr, send_sem=go_sem.at[1], recv_sem=come_sem.at[1],
        device_id=around[0], device_id_type=MESH,
    ).wait_send()
    halo_copy.wait_send()
    store.wait()
    part.wait()


def last_kernel(came_in, part, arrive_in, crm_in, dyn_out, crm_out, arrive, od, sem):
    crm = pltpu.make_async_copy(crm_in, crm_out, sem.at[0])
    load = pltpu.make_async_copy(arrive_in, arrive, sem.at[1])
    load.start()
    crm.start()
    stores = [pltpu.make_async_copy(od.at[f], dyn_out.at[f], sem.at[2 + f]) for f in range(4)]
    od[3] = part[3, :, 0:LEV]
    stores[3].start()
    lane = iota((HALO, 128), 1)
    came = came_in[...]
    came = [jnp.where(lane < 64, value, 0.0) for value in (came, pltpu.roll(came, 64, 1))]
    came = jnp.concatenate(came + [jnp.zeros((256 - 2 * HALO, 128), F32)], axis=0)
    came = jnp.concatenate(halves(came), axis=1)
    load.wait()
    taken = dot(arrive[...], came)
    for f in range(3):
        high, low = taken[128 * f : 128 * f + 128], taken[384 + 128 * f : 512 + 128 * f]
        od[f] = part[f, :, 0:LEV] + (high[:, 0:128] + high[:, 128:256] + low[:, 0:128])[:, 0:LEV]
        stores[f].start()
    crm.wait()
    for store in stores:
        store.wait()


def per_device(dyn_state, crm_state, cloud_mask, span_of):
    *consts, arrive = (jnp.asarray(value) for value in tables())
    vmem = pltpu.VMEM
    scratch = [
        vmem((4, 128, LEV), F32), vmem((3, CRM_LEV, 2048), BF16), vmem((CRM_LEV, 2048), jnp.int32),
        vmem((1, 32), jnp.int32),
    ]
    scratch += [vmem(value.shape, value.dtype) for value in consts]
    scratch += [
        vmem((8, 128), F32),
        vmem((16, 192, 128), F32), vmem((16, 192, 128), F32), vmem((16, 64, 128), F32),
        vmem((128, 128), F32),
        vmem((32, 4, 128), F32), vmem((32, 4, 128), F32),
        vmem((32, 4, 128), F32), vmem((32, 4, 128), F32),
        vmem((128, 512), F32), vmem((128, 512), F32),
        vmem((HALO, 128), F32),
        vmem((3, CRM_LEV, 2048), BF16), vmem((4, 128, 128), F32),
        vmem((96, 256), BF16), vmem((2 * HALO, 512), BF16),
        pltpu.SemaphoreType.DMA((10,)), pltpu.SemaphoreType.DMA((2,)),
        pltpu.SemaphoreType.DMA((4,)), pltpu.SemaphoreType.DMA((4,)), pltpu.SemaphoreType.DMA((GROUPS,)),
    ]
    nodes = dyn_state.transpose(0, 2, 3, 1).reshape(4, 128, LEV)
    operands = (nodes, crm_state, cloud_mask, span_of.T, *consts)
    anywhere = pl.BlockSpec(memory_space=pl.ANY)
    came, part, crm = pl.pallas_call(
        kernel,
        out_shape=(
            vmem((HALO, 128), F32), vmem((4, 128, 128), F32), vmem((3, CRM_LEV, 2048), BF16)
        ),
        in_specs=[anywhere] * 10,
        out_specs=[anywhere] * 3,
        scratch_shapes=scratch,
        compiler_params=pltpu.CompilerParams(
            collective_id=0, has_side_effects=True, vmem_limit_bytes=40 * 2**20
        ),
        name="physics_step",
    )(*(pltpu.with_memory_space_constraint(value, pltpu.HBM) for value in operands))
    near = pl.BlockSpec(memory_space=pltpu.VMEM)
    dyn, crm = pl.pallas_call(
        last_kernel,
        out_shape=(
            pltpu.HBM((4, 128, LEV), F32), pltpu.HBM((3, CRM_LEV, 2048), BF16)
        ),
        in_specs=[near, near, anywhere, anywhere],
        out_specs=[anywhere] * 2,
        scratch_shapes=[
            vmem((768, 256), BF16), vmem((4, 128, LEV), F32), pltpu.SemaphoreType.DMA((6,))
        ],
        compiler_params=pltpu.CompilerParams(vmem_limit_bytes=8 * 2**20),
        name="last_step",
    )(came, part, arrive, crm)
    return dyn.reshape(4, 16, 8, LEV).transpose(0, 3, 1, 2), crm


def solution(mesh):
    return jax.shard_map(
        per_device,
        mesh=mesh,
        in_specs=(
            P(None, None, "blk", "row"),
            P(None, None, ("blk", "row")),
            P(None, ("blk", "row")),
            P(("blk", "row"), None),
        ),
        out_specs=(P(None, None, "blk", "row"), P(None, None, ("blk", "row"))),
        check_vma=False,
    )
```

```python
import functools

import jax
import jax.numpy as jnp
import numpy as np
from jax import lax
from jax.experimental import pallas as pl
from jax.experimental.pallas import tpu as pltpu
from jax.sharding import PartitionSpec as P

MESH = pl.DeviceIdType.MESH
LEV, CRM_LEV, CRM_COLS = 72, 58, 32
F32, BF16 = jnp.float32, jnp.bfloat16
SLOTS = ((0, -1), (0, 1), (-1, 0), (1, 0), (-1, -1), (-1, 1), (1, -1), (1, 1))
STATE_ROWS = (32, 32, 16, 16, 8, 8, 8, 8)
TILES, GROUPS = 4, 4
CELL_RANK = (16, 16, 8, 8, 2, 2, 2, 2)
CELL_ROWS = (24, 24, 16, 16, 8, 8, 8, 8)
STATE_AT = tuple(int(v) for v in np.cumsum((0,) + STATE_ROWS))
CELL_AT = tuple(int(v) for v in np.cumsum((0,) + CELL_ROWS))
HALO = CELL_AT[-1]


def poly_times(first_poly, second_poly):
    product = [0.0] * (len(first_poly) + len(second_poly) - 1)
    for i, first in enumerate(first_poly):
        for j, second in enumerate(second_poly):
            product[i + j] += first * second
    return product


def poly_slope(coeffs, point):
    return sum(power * coeffs[power] * point ** (power - 1) for power in range(1, len(coeffs)))


def poly_integral(coeffs, low, high):
    return sum(
        coeffs[power] * (high ** (power + 1) - low ** (power + 1)) / (power + 1)
        for power in range(len(coeffs))
    )


def element_tables():
    root_five = float(np.sqrt(5.0))
    gll_nodes = [-1.0, -1.0 / root_five, 1.0 / root_five, 1.0]
    weights = np.array([1.0 / 6.0, 5.0 / 6.0, 5.0 / 6.0, 1.0 / 6.0])
    derivative = np.zeros((4, 4))
    to_cells = np.zeros((2, 4))
    for basis in range(4):
        coeffs = [1.0]
        for other in range(4):
            if other != basis:
                denominator = gll_nodes[basis] - gll_nodes[other]
                coeffs = poly_times(coeffs, [-gll_nodes[other] / denominator, 1.0 / denominator])
        for node in range(4):
            derivative[node, basis] = poly_slope(coeffs, gll_nodes[node])
        to_cells[0, basis] = poly_integral(coeffs, -1.0, 0.0)
        to_cells[1, basis] = poly_integral(coeffs, 0.0, 1.0)
    to_nodes = np.array([[1.0, 0.0], [1.0, 0.0], [0.0, 1.0], [0.0, 1.0]])
    edge_weights = np.array([1.0 / 3.0, 5.0 / 6.0, 5.0 / 6.0, 1.0 / 3.0])
    return derivative, weights, to_cells, to_nodes, edge_weights


def line_operators(elements):
    derivative, weights, _, _, edge_weights = element_tables()
    count = elements * 4 * 3
    weight = np.tile(weights, elements * 3)
    fold = np.eye(count)
    for node in range(count):
        if node % 4 == 0:
            fold[node, (node - 1) % count] += 1.0
        if node % 4 == 3:
            fold[node, (node + 1) % count] += 1.0
    fold = fold / np.tile(edge_weights, elements * 3)[:, None]
    smooth = fold * weight
    stiff = np.kron(np.eye(elements * 3), derivative.T @ np.diag(weights) @ derivative)
    mine = slice(elements * 4, elements * 8)
    return smooth[mine], (fold @ stiff @ smooth)[mine], (smooth @ smooth)[mine]


def split(value):
    high = np.asarray(value, np.float32).astype(jnp.bfloat16)
    return high, (np.asarray(value, np.float32) - high.astype(np.float32)).astype(jnp.bfloat16)


@functools.cache
def tables():
    _, _, to_cells, to_nodes, _ = element_tables()
    smooth_x, stiff_x, mass_x = line_operators(4)
    smooth_y, stiff_y, mass_y = line_operators(2)
    nodes = np.kron(np.kron(np.eye(4), to_nodes), np.kron(np.eye(2), to_nodes))

    def block(dx, dy):
        x, y = slice(16 * (dx + 1), 16 * (dx + 2)), slice(8 * (dy + 1), 8 * (dy + 2))
        return np.kron(smooth_x[:, x], smooth_y[:, y]) - 0.01 * (
            np.kron(stiff_x[:, x], mass_y[:, y]) + np.kron(mass_x[:, x], stiff_y[:, y])
        )

    cell_sums = np.zeros((32, 128))
    cell_sums[:] = np.kron(np.kron(np.eye(4), to_cells), np.kron(np.eye(2), to_cells))
    mine = block(0, 0)
    own = np.zeros((128, 128))
    own[:, :32] = mine @ nodes
    outer, inner = np.zeros((128, 128)), np.zeros((128, 128))
    arrive = np.zeros((3, 128, 256))
    leave = np.zeros((2, HALO, 128))
    pick = np.zeros((HALO, 256), np.float32)
    for slot, (dx, dy) in enumerate(SLOTS):
        part = block(dx, dy)
        left, scale, right = np.linalg.svd(part)
        rank = int((scale > 1e-10).sum())
        assert rank <= STATE_ROWS[slot]
        at = STATE_AT[slot]
        outer[:, at : at + rank] = left[:, :rank] * np.sqrt(scale[:rank])
        inner[at : at + rank] = right[:rank] * np.sqrt(scale[:rank])[:, None]
        left, scale, right = np.linalg.svd(part @ nodes, full_matrices=False)
        rank = int((scale > 1e-10).sum())
        assert rank <= CELL_RANK[slot]
        left, right = left * np.sqrt(scale), right * np.sqrt(scale)[:, None]
        half = CELL_RANK[slot] // 2
        for field in range(3):
            at = CELL_AT[slot] + field * half
            pick[at : at + half, field::4] = 1.0
            for h in range(2):
                leave[h, at : at + half, :32] = right[h : 2 * half : 2]
                arrive[field, :, h * HALO + at : h * HALO + at + half] = left[:, h : 2 * half : 2]
    pieces = []
    for matrix in (inner, mine, outer, own, leave[0], leave[1]):
        pieces.extend(split(matrix))
    matrices = np.concatenate(pieces, axis=0)
    cell_sums = np.concatenate(split(cell_sums), axis=0)
    arrive = np.concatenate(split(arrive.reshape(384, 256)), axis=0)

    cell = np.arange(128)
    same = (cell[:, None] // 32) == (cell[None, :] // 32)
    step = (cell[:, None] - cell[None, :]) % 32
    east, west = same & (step == 1), same & (step == 31)
    along = np.concatenate([1.0 * east + 1.0 * west - same / 16.0, 1.0 * east - 1.0 * west], axis=1)
    along = np.concatenate([along, along], axis=0).astype(jnp.bfloat16)

    spread = np.zeros((16, 384))
    for s in range(2):
        for pair in range(2):
            for field in range(3):
                at = field * 128 + pair * 64 + s * 32
                spread[s * 8 + pair * 4 + field, at : at + 32] = 1.0
    means = (spread / 32.0).astype(jnp.bfloat16)
    spread = np.concatenate([spread, spread, np.zeros((96, 384))], axis=0).astype(jnp.bfloat16)
    return cell_sums, matrices, along, spread, means, pick, arrive


def halves(value):
    high = value.astype(BF16)
    return high, (value - high.astype(F32)).astype(BF16)


def dot(left, right):
    return jnp.dot(left, right, preferred_element_type=F32)


def dot_split(left, right):
    high, low = halves(right)
    return dot(left[0], high) + dot(left[1], high) + dot(left[0], low)


def slot_means(weights, fields):
    return lax.dot_general(
        weights, fields, (((1,), (1,)), ((), ())), preferred_element_type=F32
    )


def iota(shape, axis):
    return lax.broadcasted_iota(jnp.int32, shape, axis)


def levels_moved(field):
    sub = iota((8, 128), 0)
    rows = [field[8 * k : 8 * k + 8] for k in range(8)]
    up = [pltpu.roll(value, 7, 0) for value in rows]
    down = [pltpu.roll(value, 1, 0) for value in rows]
    moved = []
    for k in range(8):
        above = jnp.where(sub == 7, up[k + 1], up[k]) if k < 7 else jnp.where(sub >= 1, rows[7], up[7])
        below = jnp.where(sub == 0, down[k - 1] if k else rows[0], down[k])
        moved.append(above + below)
    return jnp.concatenate(moved, axis=0)


def transported(field, along, momentum):
    return (
        0.4 * field
        + 0.15 * (along[:, :128] + levels_moved(field))
        + momentum * along[:, 128:]
    )


def condensed(heat, water, wet, saturation):
    cond = wet * jnp.maximum(water - 0.5 * heat - saturation, 0.0)
    return heat + 0.8 * cond, water - cond


def kernel(
    dyn, crm, mask, span, sums_in, matrices, along_in, spread_in, means_in, pick_in,
    hr, part_out, crm_out,
    xin, xb, mk, sp, sums, mat, along, spread, means, pick,
    spans, xs, ys, wt, cat, og, ar, rs, rt, dh, dr, hs, ob, od, place, post,
    load_sem, store_sem, go_sem, come_sem, tile_sem,
):
    p, r = lax.axis_index("blk"), lax.axis_index("row")
    rows, blocks = lax.axis_size("row"), lax.axis_size("blk")
    barrier = pltpu.get_barrier_semaphore()

    def far_first(k):
        return lax.rem(r + 16 + (1 - 2 * (k & 1)) * ((k + 1) >> 1), rows)

    def greet(k, carry):
        pl.semaphore_signal(barrier, inc=1, device_id=(p, far_first(k)), device_id_type=MESH)
        return carry

    lax.fori_loop(0, rows - 1, greet, None)
    around = [
        (lax.rem(p + blocks - dx, blocks), lax.rem(r + rows - dy, rows)) for dx, dy in SLOTS
    ]
    for slot in range(2, 8):
        pl.semaphore_signal(barrier, inc=1, device_id=around[slot], device_id_type=MESH)

    loads = [
        pltpu.make_async_copy(source, target, load_sem.at[k])
        for k, (source, target) in enumerate(
            ((span, sp), (sums_in, sums), (dyn, xin), (crm, xb), (mask, mk), (along_in, along),
             (spread_in, spread), (means_in, means), (matrices, mat), (pick_in, pick))
        )
    ]
    for load in loads[:3]:
        load.start()

    cat[...] = jnp.zeros_like(cat)
    spans[...] = jnp.zeros_like(spans)

    def table(k, lines=128):
        at = (0, 256, 512, 768, 1024, 1024 + 2 * HALO)[k]
        return mat[at : at + lines], mat[at + lines : at + 2 * lines]

    loads[0].wait()
    spans[0:1, 0:32] = sp[...].astype(F32)
    named = spans[...]
    named = named + pltpu.roll(named, 32, 1)
    named = named + pltpu.roll(named, 64, 1)
    lane, line = iota((32, 128), 1), iota((32, 128), 0)
    across = jnp.broadcast_to(named[0:1, :], (32, 128))
    down = jnp.sum(jnp.where(lane == line, across, 0.0), axis=1, keepdims=True)
    earlier = jnp.where((down == across) & (line < (lane & 31)), 1.0, 0.0)
    position = 2.0 * named[0:1, :] + jnp.sum(earlier, axis=0, keepdims=True)
    lane, line = iota((128, 128), 1), iota((128, 128), 0)
    wanted = (2 * line - (line & 3)).astype(F32)
    offered = 4.0 * jnp.broadcast_to(position, (128, 128)) + (lane >> 5).astype(F32)
    send_to = jnp.concatenate(
        [jnp.where(offered - 4.0 * s == wanted, 1.0, 0.0) for s in range(2)], axis=1
    ).astype(BF16)

    loads[1].wait()
    loads[2].wait()
    for load in loads[3:6]:
        load.start()
    for field in range(3):
        cat[32 * field : 32 * field + 32, 0:LEV] = dot_split((sums[0:32], sums[32:64]), xin[field])
    first = jnp.where(lane < CRM_LEV, cat[...], 0.0)
    high, low = halves(jnp.concatenate([first, pltpu.roll(first, 64, 1)], axis=0))
    sent = dot(send_to, jnp.concatenate([high, low], axis=1))
    og[...] = (sent[:, :128] + sent[:, 128:]).reshape(32, 4, 128)

    pl.semaphore_wait(barrier, rows - 1 + 6)

    def profile_copy(target):
        return pltpu.make_async_remote_copy(
            src_ref=og.at[target], dst_ref=ar.at[r], send_sem=go_sem.at[0],
            recv_sem=tile_sem.at[lax.div(r, 2 * TILES)], device_id=(p, target), device_id_type=MESH,
        )

    def send_profile(k, carry):
        away = (1 - 2 * (k & 1)) * ((k + 2) >> 1)
        profile_copy(lax.rem(r + rows + away, rows)).start()
        return carry

    lax.fori_loop(0, rows - 1, send_profile, None)
    ar[r] = og[r]

    for load in loads[6:]:
        load.start()

    for k in range(3, 6):
        loads[k].wait()
    row = iota((64, 128), 0)
    saturation = 0.5 - row.astype(F32) / CRM_LEV
    rest = jnp.zeros((64 - CRM_LEV, 128), F32)

    def begin(group, carry):
        first = pl.multiple_of(group * TILES, TILES)
        state = []
        for t in range(TILES):
            at = pl.ds(pl.multiple_of(128 * (first + t), 128), 128)
            wt[first + t] = jnp.concatenate([0.5 * mk[:, at].astype(F32), rest], axis=0)
            for f in range(3):
                state.append(jnp.concatenate([xb[f, :, at].astype(F32), rest], axis=0))
        shifted = dot(jnp.concatenate(state, axis=0).astype(BF16), along[0:128, :])
        for t in range(TILES):
            momentum = -0.1 * state[3 * t + 2]
            for f in range(3):
                line = 64 * (3 * t + f)
                moved = transported(state[3 * t + f], shifted[line : line + 64], momentum)
                ys[first + t, 64 * f : 64 * f + 64, :] = moved
        start = jnp.concatenate(
            [jnp.concatenate(state[3 * t : 3 * t + 3], axis=1) for t in range(TILES)], axis=0
        )
        mean = slot_means(means[...], start.astype(BF16))
        for t in range(TILES):
            part = mean[:, 64 * t : 64 * t + 64]
            xs[first + t] = jnp.concatenate([part[0:8], part[8:16]], axis=1)
        return carry

    loads[7].wait()
    lax.fori_loop(0, GROUPS, begin, None)
    loads[6].wait()

    def all_of(source, target, k):
        return pltpu.make_async_remote_copy(
            src_ref=source.at[pl.ds(0, 31)], dst_ref=target.at[pl.ds(0, 31)],
            send_sem=go_sem.at[k], recv_sem=come_sem.at[k],
            device_id=(p, lax.rem(r + 1, rows)), device_id_type=MESH,
        )

    def tendency_copy(target):
        return pltpu.make_async_remote_copy(
            src_ref=rs.at[target], dst_ref=rt.at[r], send_sem=go_sem.at[2],
            recv_sem=come_sem.at[2], device_id=(p, target), device_id_type=MESH,
        )

    mine = lax.div(r, 2 * TILES)

    def finish(group, own):
        first = pl.multiple_of(group * TILES, TILES)
        near = ar.at[pl.ds(2 * first, 2 * TILES)]
        due = ar.at[pl.ds(2 * first, 2 * TILES - own)]
        pltpu.make_async_copy(due, due, tile_sem.at[group]).wait()
        near = 0.3 * near[...].reshape(8 * TILES, 128)
        parts = [part.astype(F32) for part in (*halves(near), *halves(pltpu.roll(near, 64, 1)))]
        near = jnp.concatenate(
            [parts[k][8 * t : 8 * t + 8] for t in range(TILES) for k in (0, 2, 1, 3)], axis=0
        ).T[0:64]
        near = [near] + [pltpu.roll(near, 128 - 32 * t, 1) for t in range(1, TILES)]
        pulled = dot(jnp.concatenate(near, axis=0).astype(BF16), spread[...])
        pulled = [
            [pulled[64 * t : 64 * t + 64, 128 * f : 128 * f + 128] for f in range(3)]
            for t in range(TILES)
        ]
        fields = []
        for t in range(TILES):
            one = [ys[first + t, 64 * f : 64 * f + 64, :] + pulled[t][f] for f in range(3)]
            one[0], one[1] = condensed(one[0], one[1], wt[first + t], saturation)
            fields.append(one)
        both = [jnp.concatenate(halves(value), axis=1) for one in fields for value in one]
        shifted = dot(jnp.concatenate(both, axis=0), along[...])
        change = []
        for t in range(TILES):
            at = pl.ds(pl.multiple_of(128 * (first + t), 128), 128)
            one = fields[t]
            momentum = -0.1 * one[2]
            two = []
            for f in range(3):
                line = 64 * (3 * t + f)
                moved = transported(one[f], shifted[line : line + 64], momentum)
                two.append(moved + pulled[t][f])
            two[0], two[1] = condensed(two[0], two[1], wt[first + t], saturation)
            parts = []
            for f in range(3):
                parts.append(halves(two[f]))
                ob[f, :, at] = parts[f][0][0:CRM_LEV]
            change += [jnp.concatenate([part[h] for part in parts], axis=1) for h in range(2)]
        mean = slot_means(means[...], jnp.concatenate(change, axis=0))
        for t in range(TILES):
            part = mean[:, 128 * t : 128 * t + 128]
            part = part + pltpu.roll(part, 64, 1)
            message = jnp.where(iota((8, 128), 1) < 64, part[0:8], part[8:16]) - xs[first + t]
            for pair in range(2):
                rs[2 * (first + t) + pair] = message[4 * pair : 4 * pair + 4]
        for k in range(2 * TILES):
            target = 2 * first + k
            if own:
                pl.when(target != r)(tendency_copy(target).start)
            else:
                tendency_copy(target).start()

    def others(k, carry):
        away = (1 - 2 * (k & 1)) * ((k + 2) >> 1)
        finish(lax.rem(mine + GROUPS + away, GROUPS), 0)
        return carry

    lax.fori_loop(0, GROUPS - 1, others, None)
    finish(mine, 1)
    rt[r] = rs[r]

    store = pltpu.make_async_copy(ob, crm_out, store_sem.at[0])
    store.start()

    loads[8].wait()
    for field in range(4):
        dh[:, 128 * field : 128 * field + LEV] = dot_split(table(0), xin[field])
    state_copies = []
    for slot in range(8):
        at = pl.ds(STATE_AT[slot], STATE_ROWS[slot])
        state_copies.append(
            pltpu.make_async_remote_copy(
                src_ref=dh.at[at], dst_ref=dr.at[at], send_sem=go_sem.at[1],
                recv_sem=come_sem.at[1], device_id=around[slot], device_id_type=MESH,
            )
        )
        state_copies[-1].start()

    loads[9].wait()
    lane, line = iota((32, 128), 1), iota((32, 128), 0)
    home = jnp.sum(
        jnp.where(lane == line, jnp.broadcast_to(position, (32, 128)), 0.0), axis=1, keepdims=True
    )
    code = (lane >> 2).astype(F32)
    match = jnp.concatenate(
        [jnp.where(home - s == 2.0 * code, 1.0, 0.0) for s in range(2)], axis=1
    )
    lane = iota((32, 256), 1)
    for field in range(3):
        place[32 * field : 32 * field + 32, :] = jnp.where((lane & 3) == field, match, 0.0).astype(BF16)
    match = match.astype(BF16)
    for h in range(2):
        for half, piece in enumerate(table(4 + h, HALO)):
            at = (2 * half + h) * HALO
            post[at : at + HALO, :] = (
                pick[...] * dot(piece[:, 0:32], match)
            ).astype(BF16)

    for field in range(4):
        od[field, :, 0:LEV] = dot_split(table(1), xin[field])

    all_of(rs, rt, 2).wait_recv()
    given = rt[...].reshape(128, 128)
    lane = iota((128, 128), 1)
    given = [jnp.where(lane < CRM_LEV, value, 0.0) for value in (given, pltpu.roll(given, 64, 1))]
    given = jnp.concatenate(halves(jnp.concatenate(given, axis=0)), axis=1)
    sent = dot(post[...], given)
    sent = [sent[HALO * k : HALO * k + HALO] for k in range(4)]
    sent = [sent[h][:, 0:128] + sent[h][:, 128:256] + sent[2 + h][:, 0:128] for h in range(2)]
    hs[...] = sent[0] + pltpu.roll(sent[1], 64, 1)
    cell_copies = []
    for slot in range(8):
        at = pl.ds(CELL_AT[slot], CELL_ROWS[slot])
        cell_copies.append(
            pltpu.make_async_remote_copy(
                src_ref=hs.at[at], dst_ref=hr.at[at], send_sem=go_sem.at[3],
                recv_sem=come_sem.at[3], device_id=around[slot], device_id_type=MESH,
            )
        )
        cell_copies[-1].start()
    cells = dot(place[...], given)
    cells = cells[:, 0:128] + cells[:, 128:256]
    own = table(3)
    own = own[0][:, 0:32], own[1][:, 0:32]
    for field in range(3):
        od[field, :, 0:LEV] += dot_split(own, cells[32 * field : 32 * field + 32])[:, 0:LEV]

    pltpu.make_async_remote_copy(
        src_ref=dh, dst_ref=dr, send_sem=go_sem.at[1], recv_sem=come_sem.at[1],
        device_id=around[0], device_id_type=MESH,
    ).wait_recv()
    for field in range(4):
        od[field, :, 0:LEV] += dot_split(table(2), dr[:, 128 * field : 128 * field + 128])[:, 0:LEV]

    halo_copy = pltpu.make_async_remote_copy(
        src_ref=hs, dst_ref=hr, send_sem=go_sem.at[3],
        recv_sem=come_sem.at[3], device_id=around[0], device_id_type=MESH,
    )
    part = pltpu.make_async_copy(od, part_out, store_sem.at[1])
    part.start()
    halo_copy.wait_recv()
    all_of(og, ar, 0).wait_send()
    all_of(rs, rt, 2).wait_send()
    pltpu.make_async_remote_copy(
        src_ref=dh, dst_ref=dr, send_sem=go_sem.at[1], recv_sem=come_sem.at[1],
        device_id=around[0], device_id_type=MESH,
    ).wait_send()
    halo_copy.wait_send()
    store.wait()
    part.wait()


def last_kernel(came_in, part, arrive_in, crm_in, dyn_out, crm_out, arrive, od, sem):
    crm = pltpu.make_async_copy(crm_in, crm_out, sem.at[0])
    load = pltpu.make_async_copy(arrive_in, arrive, sem.at[1])
    load.start()
    crm.start()
    stores = [pltpu.make_async_copy(od.at[f], dyn_out.at[f], sem.at[2 + f]) for f in range(4)]
    od[3] = part[3, :, 0:LEV]
    stores[3].start()
    lane = iota((HALO, 128), 1)
    came = came_in[...]
    came = [jnp.where(lane < 64, value, 0.0) for value in (came, pltpu.roll(came, 64, 1))]
    came = jnp.concatenate(came + [jnp.zeros((256 - 2 * HALO, 128), F32)], axis=0)
    came = jnp.concatenate(halves(came), axis=1)
    load.wait()
    taken = dot(arrive[...], came)
    for f in range(3):
        high, low = taken[128 * f : 128 * f + 128], taken[384 + 128 * f : 512 + 128 * f]
        od[f] = part[f, :, 0:LEV] + (high[:, 0:128] + high[:, 128:256] + low[:, 0:128])[:, 0:LEV]
        stores[f].start()
    crm.wait()
    for store in stores:
        store.wait()


def per_device(dyn_state, crm_state, cloud_mask, span_of):
    *consts, arrive = (jnp.asarray(value) for value in tables())
    vmem = pltpu.VMEM
    scratch = [
        vmem((4, 128, LEV), F32), vmem((3, CRM_LEV, 2048), BF16), vmem((CRM_LEV, 2048), jnp.int32),
        vmem((1, 32), jnp.int32),
    ]
    scratch += [vmem(value.shape, value.dtype) for value in consts]
    scratch += [
        vmem((8, 128), F32),
        vmem((16, 8, 128), F32), vmem((16, 192, 128), F32), vmem((16, 64, 128), F32),
        vmem((128, 128), F32),
        vmem((32, 4, 128), F32), vmem((32, 4, 128), F32),
        vmem((32, 4, 128), F32), vmem((32, 4, 128), F32),
        vmem((128, 512), F32), vmem((128, 512), F32),
        vmem((HALO, 128), F32),
        vmem((3, CRM_LEV, 2048), BF16), vmem((4, 128, 128), F32),
        vmem((96, 256), BF16), vmem((4 * HALO, 256), BF16),
        pltpu.SemaphoreType.DMA((10,)), pltpu.SemaphoreType.DMA((2,)),
        pltpu.SemaphoreType.DMA((4,)), pltpu.SemaphoreType.DMA((4,)), pltpu.SemaphoreType.DMA((GROUPS,)),
    ]
    nodes = dyn_state.transpose(0, 2, 3, 1).reshape(4, 128, LEV)
    operands = (nodes, crm_state, cloud_mask, span_of.T, *consts)
    anywhere = pl.BlockSpec(memory_space=pl.ANY)
    came, part, crm = pl.pallas_call(
        kernel,
        out_shape=(
            vmem((HALO, 128), F32), vmem((4, 128, 128), F32), vmem((3, CRM_LEV, 2048), BF16)
        ),
        in_specs=[anywhere] * 10,
        out_specs=[anywhere] * 3,
        scratch_shapes=scratch,
        compiler_params=pltpu.CompilerParams(
            collective_id=0, has_side_effects=True, vmem_limit_bytes=40 * 2**20
        ),
        name="physics_step",
    )(*(pltpu.with_memory_space_constraint(value, pltpu.HBM) for value in operands))
    near = pl.BlockSpec(memory_space=pltpu.VMEM)
    dyn, crm = pl.pallas_call(
        last_kernel,
        out_shape=(
            pltpu.HBM((4, 128, LEV), F32), pltpu.HBM((3, CRM_LEV, 2048), BF16)
        ),
        in_specs=[near, near, anywhere, anywhere],
        out_specs=[anywhere] * 2,
        scratch_shapes=[
            vmem((768, 256), BF16), vmem((4, 128, LEV), F32), pltpu.SemaphoreType.DMA((6,))
        ],
        compiler_params=pltpu.CompilerParams(vmem_limit_bytes=8 * 2**20),
        name="last_step",
    )(came, part, arrive, crm)
    return dyn.reshape(4, 16, 8, LEV).transpose(0, 3, 1, 2), crm


def solution(mesh):
    return jax.shard_map(
        per_device,
        mesh=mesh,
        in_specs=(
            P(None, None, "blk", "row"),
            P(None, None, ("blk", "row")),
            P(None, ("blk", "row")),
            P(("blk", "row"), None),
        ),
        out_specs=(P(None, None, "blk", "row"), P(None, None, ("blk", "row"))),
        check_vma=False,
    )
```

```python
import functools

import jax
import jax.numpy as jnp
import numpy as np
from jax import lax
from jax.experimental import pallas as pl
from jax.experimental.pallas import tpu as pltpu
from jax.sharding import PartitionSpec as P

MESH = pl.DeviceIdType.MESH
LEV, CRM_LEV, CRM_COLS = 72, 58, 32
F32, BF16 = jnp.float32, jnp.bfloat16
SLOTS = ((0, -1), (0, 1), (-1, 0), (1, 0), (-1, -1), (-1, 1), (1, -1), (1, 1))
STATE_ROWS = (32, 32, 16, 16, 8, 8, 8, 8)
TILES, GROUPS = 4, 4
CELL_RANK = (16, 16, 8, 8, 2, 2, 2, 2)
CELL_ROWS = (24, 24, 16, 16, 8, 8, 8, 8)
STATE_AT = tuple(int(v) for v in np.cumsum((0,) + STATE_ROWS))
CELL_AT = tuple(int(v) for v in np.cumsum((0,) + CELL_ROWS))
HALO = CELL_AT[-1]


def poly_times(first_poly, second_poly):
    product = [0.0] * (len(first_poly) + len(second_poly) - 1)
    for i, first in enumerate(first_poly):
        for j, second in enumerate(second_poly):
            product[i + j] += first * second
    return product


def poly_slope(coeffs, point):
    return sum(power * coeffs[power] * point ** (power - 1) for power in range(1, len(coeffs)))


def poly_integral(coeffs, low, high):
    return sum(
        coeffs[power] * (high ** (power + 1) - low ** (power + 1)) / (power + 1)
        for power in range(len(coeffs))
    )


def element_tables():
    root_five = float(np.sqrt(5.0))
    gll_nodes = [-1.0, -1.0 / root_five, 1.0 / root_five, 1.0]
    weights = np.array([1.0 / 6.0, 5.0 / 6.0, 5.0 / 6.0, 1.0 / 6.0])
    derivative = np.zeros((4, 4))
    to_cells = np.zeros((2, 4))
    for basis in range(4):
        coeffs = [1.0]
        for other in range(4):
            if other != basis:
                denominator = gll_nodes[basis] - gll_nodes[other]
                coeffs = poly_times(coeffs, [-gll_nodes[other] / denominator, 1.0 / denominator])
        for node in range(4):
            derivative[node, basis] = poly_slope(coeffs, gll_nodes[node])
        to_cells[0, basis] = poly_integral(coeffs, -1.0, 0.0)
        to_cells[1, basis] = poly_integral(coeffs, 0.0, 1.0)
    to_nodes = np.array([[1.0, 0.0], [1.0, 0.0], [0.0, 1.0], [0.0, 1.0]])
    edge_weights = np.array([1.0 / 3.0, 5.0 / 6.0, 5.0 / 6.0, 1.0 / 3.0])
    return derivative, weights, to_cells, to_nodes, edge_weights


def line_operators(elements):
    derivative, weights, _, _, edge_weights = element_tables()
    count = elements * 4 * 3
    weight = np.tile(weights, elements * 3)
    fold = np.eye(count)
    for node in range(count):
        if node % 4 == 0:
            fold[node, (node - 1) % count] += 1.0
        if node % 4 == 3:
            fold[node, (node + 1) % count] += 1.0
    fold = fold / np.tile(edge_weights, elements * 3)[:, None]
    smooth = fold * weight
    stiff = np.kron(np.eye(elements * 3), derivative.T @ np.diag(weights) @ derivative)
    mine = slice(elements * 4, elements * 8)
    return smooth[mine], (fold @ stiff @ smooth)[mine], (smooth @ smooth)[mine]


def split(value):
    high = np.asarray(value, np.float32).astype(jnp.bfloat16)
    return high, (np.asarray(value, np.float32) - high.astype(np.float32)).astype(jnp.bfloat16)


@functools.cache
def tables():
    _, _, to_cells, to_nodes, _ = element_tables()
    smooth_x, stiff_x, mass_x = line_operators(4)
    smooth_y, stiff_y, mass_y = line_operators(2)
    nodes = np.kron(np.kron(np.eye(4), to_nodes), np.kron(np.eye(2), to_nodes))

    def block(dx, dy):
        x, y = slice(16 * (dx + 1), 16 * (dx + 2)), slice(8 * (dy + 1), 8 * (dy + 2))
        return np.kron(smooth_x[:, x], smooth_y[:, y]) - 0.01 * (
            np.kron(stiff_x[:, x], mass_y[:, y]) + np.kron(mass_x[:, x], stiff_y[:, y])
        )

    cell_sums = np.zeros((32, 128))
    cell_sums[:] = np.kron(np.kron(np.eye(4), to_cells), np.kron(np.eye(2), to_cells))
    mine = block(0, 0)
    own = np.zeros((128, 128))
    own[:, :32] = mine @ nodes
    outer, inner = np.zeros((128, 128)), np.zeros((128, 128))
    arrive = np.zeros((3, 128, 256))
    leave = np.zeros((2, HALO, 128))
    pick = np.zeros((HALO, 256), np.float32)
    for slot, (dx, dy) in enumerate(SLOTS):
        part = block(dx, dy)
        left, scale, right = np.linalg.svd(part)
        rank = int((scale > 1e-10).sum())
        assert rank <= STATE_ROWS[slot]
        at = STATE_AT[slot]
        outer[:, at : at + rank] = left[:, :rank] * np.sqrt(scale[:rank])
        inner[at : at + rank] = right[:rank] * np.sqrt(scale[:rank])[:, None]
        left, scale, right = np.linalg.svd(part @ nodes, full_matrices=False)
        rank = int((scale > 1e-10).sum())
        assert rank <= CELL_RANK[slot]
        left, right = left * np.sqrt(scale), right * np.sqrt(scale)[:, None]
        half = CELL_RANK[slot] // 2
        for field in range(3):
            at = CELL_AT[slot] + field * half
            pick[at : at + half, field::4] = 1.0
            for h in range(2):
                leave[h, at : at + half, :32] = right[h : 2 * half : 2]
                arrive[field, :, h * HALO + at : h * HALO + at + half] = left[:, h : 2 * half : 2]
    pieces = []
    for matrix in (inner, mine, outer, own, leave[0], leave[1]):
        pieces.extend(split(matrix))
    matrices = np.concatenate(pieces, axis=0)
    cell_sums = np.concatenate(split(cell_sums), axis=0)
    arrive = np.concatenate(split(arrive.reshape(384, 256)), axis=0)

    cell = np.arange(128)
    same = (cell[:, None] // 32) == (cell[None, :] // 32)
    step = (cell[:, None] - cell[None, :]) % 32
    east, west = same & (step == 1), same & (step == 31)
    along = np.concatenate([1.0 * east + 1.0 * west - same / 16.0, 1.0 * east - 1.0 * west], axis=1)
    along = np.concatenate([along, along], axis=0).astype(jnp.bfloat16)

    spread = np.zeros((16, 384))
    for s in range(2):
        for pair in range(2):
            for field in range(3):
                at = field * 128 + pair * 64 + s * 32
                spread[s * 8 + pair * 4 + field, at : at + 32] = 1.0
    means = (spread / 32.0).astype(jnp.bfloat16)
    spread = np.concatenate([spread, spread, np.zeros((96, 384))], axis=0).astype(jnp.bfloat16)
    return cell_sums, matrices, along, spread, means, pick, arrive


def halves(value):
    high = value.astype(BF16)
    return high, (value - high.astype(F32)).astype(BF16)


def dot(left, right):
    return jnp.dot(left, right, preferred_element_type=F32)


def dot_split(left, right):
    high, low = halves(right)
    return dot(left[0], high) + dot(left[1], high) + dot(left[0], low)


def slot_means(weights, fields):
    return lax.dot_general(
        weights, fields, (((1,), (1,)), ((), ())), preferred_element_type=F32
    )


def iota(shape, axis):
    return lax.broadcasted_iota(jnp.int32, shape, axis)


def levels_moved(field):
    sub = iota((8, 128), 0)
    rows = [field[8 * k : 8 * k + 8] for k in range(8)]
    up = [pltpu.roll(value, 7, 0) for value in rows]
    down = [pltpu.roll(value, 1, 0) for value in rows]
    moved = []
    for k in range(8):
        above = jnp.where(sub == 7, up[k + 1], up[k]) if k < 7 else jnp.where(sub >= 1, rows[7], up[7])
        below = jnp.where(sub == 0, down[k - 1] if k else rows[0], down[k])
        moved.append(above + below)
    return jnp.concatenate(moved, axis=0)


def transported(field, along, momentum):
    return (
        0.4 * field
        + 0.15 * (along[:, :128] + levels_moved(field))
        + momentum * along[:, 128:]
    )


def condensed(heat, water, wet, saturation):
    cond = wet * jnp.maximum(water - 0.5 * heat - saturation, 0.0)
    return heat + 0.8 * cond, water - cond


def kernel(
    dyn, crm, mask, span, sums_in, matrices, along_in, spread_in, means_in, pick_in,
    hr, part_out, crm_out,
    xin, xb, mk, sp, sums, mat, along, spread, means, pick,
    spans, xs, ys, wt, cat, og, ar, rs, rt, dh, dr, hs, ob, od, place, post,
    load_sem, store_sem, go_sem, come_sem, tile_sem,
):
    p, r = lax.axis_index("blk"), lax.axis_index("row")
    rows, blocks = lax.axis_size("row"), lax.axis_size("blk")
    barrier = pltpu.get_barrier_semaphore()

    def far_first(k):
        return lax.rem(r + 16 + (1 - 2 * (k & 1)) * ((k + 1) >> 1), rows)

    def greet(k, carry):
        pl.semaphore_signal(barrier, inc=1, device_id=(p, far_first(k)), device_id_type=MESH)
        return carry

    lax.fori_loop(0, rows - 1, greet, None, unroll=True)
    around = [
        (lax.rem(p + blocks - dx, blocks), lax.rem(r + rows - dy, rows)) for dx, dy in SLOTS
    ]
    for slot in range(2, 8):
        pl.semaphore_signal(barrier, inc=1, device_id=around[slot], device_id_type=MESH)

    loads = [
        pltpu.make_async_copy(source, target, load_sem.at[k])
        for k, (source, target) in enumerate(
            ((span, sp), (sums_in, sums), (dyn, xin), (crm, xb), (mask, mk), (along_in, along),
             (spread_in, spread), (means_in, means), (matrices, mat), (pick_in, pick))
        )
    ]
    for load in loads[:3]:
        load.start()

    cat[...] = jnp.zeros_like(cat)
    spans[...] = jnp.zeros_like(spans)

    def table(k, lines=128):
        at = (0, 256, 512, 768, 1024, 1024 + 2 * HALO)[k]
        return mat[at : at + lines], mat[at + lines : at + 2 * lines]

    loads[0].wait()
    spans[0:1, 0:32] = sp[...].astype(F32)
    named = spans[...]
    named = named + pltpu.roll(named, 32, 1)
    named = named + pltpu.roll(named, 64, 1)
    lane, line = iota((32, 128), 1), iota((32, 128), 0)
    across = jnp.broadcast_to(named[0:1, :], (32, 128))
    down = jnp.sum(jnp.where(lane == line, across, 0.0), axis=1, keepdims=True)
    earlier = jnp.where((down == across) & (line < (lane & 31)), 1.0, 0.0)
    position = 2.0 * named[0:1, :] + jnp.sum(earlier, axis=0, keepdims=True)
    lane, line = iota((128, 128), 1), iota((128, 128), 0)
    wanted = (2 * line - (line & 3)).astype(F32)
    offered = 4.0 * jnp.broadcast_to(position, (128, 128)) + (lane >> 5).astype(F32)
    send_to = jnp.concatenate(
        [jnp.where(offered - 4.0 * s == wanted, 1.0, 0.0) for s in range(2)], axis=1
    ).astype(BF16)

    loads[1].wait()
    loads[2].wait()
    for load in loads[3:6]:
        load.start()
    for field in range(3):
        cat[32 * field : 32 * field + 32, 0:LEV] = dot_split((sums[0:32], sums[32:64]), xin[field])
    first = jnp.where(lane < CRM_LEV, cat[...], 0.0)
    high, low = halves(jnp.concatenate([first, pltpu.roll(first, 64, 1)], axis=0))
    sent = dot(send_to, jnp.concatenate([high, low], axis=1))
    og[...] = (sent[:, :128] + sent[:, 128:]).reshape(32, 4, 128)

    pl.semaphore_wait(barrier, rows - 1 + 6)

    def profile_copy(target):
        return pltpu.make_async_remote_copy(
            src_ref=og.at[target], dst_ref=ar.at[r], send_sem=go_sem.at[0],
            recv_sem=tile_sem.at[lax.div(r, 2 * TILES)], device_id=(p, target), device_id_type=MESH,
        )

    def send_profile(k, carry):
        profile_copy(far_first(k)).start()
        return carry

    lax.fori_loop(0, rows - 1, send_profile, None, unroll=True)
    ar[r] = og[r]

    for load in loads[6:]:
        load.start()

    for k in range(3, 6):
        loads[k].wait()
    row = iota((64, 128), 0)
    saturation = 0.5 - row.astype(F32) / CRM_LEV
    rest = jnp.zeros((64 - CRM_LEV, 128), F32)

    def begin(group, carry):
        first = pl.multiple_of(group * TILES, TILES)
        state = []
        for t in range(TILES):
            at = pl.ds(pl.multiple_of(128 * (first + t), 128), 128)
            wt[first + t] = jnp.concatenate([0.5 * mk[:, at].astype(F32), rest], axis=0)
            for f in range(3):
                state.append(jnp.concatenate([xb[f, :, at].astype(F32), rest], axis=0))
        shifted = dot(jnp.concatenate(state, axis=0).astype(BF16), along[0:128, :])
        for t in range(TILES):
            momentum = -0.1 * state[3 * t + 2]
            for f in range(3):
                line = 64 * (3 * t + f)
                moved = transported(state[3 * t + f], shifted[line : line + 64], momentum)
                ys[first + t, 64 * f : 64 * f + 64, :] = moved
        start = jnp.concatenate(
            [jnp.concatenate(state[3 * t : 3 * t + 3], axis=1) for t in range(TILES)], axis=0
        )
        mean = slot_means(means[...], start.astype(BF16))
        for t in range(TILES):
            part = mean[:, 64 * t : 64 * t + 64]
            xs[first + t] = jnp.concatenate([part[0:8], part[8:16]], axis=1)
        return carry

    loads[7].wait()
    lax.fori_loop(0, GROUPS, begin, None)
    loads[6].wait()

    def all_of(source, target, k):
        return pltpu.make_async_remote_copy(
            src_ref=source.at[pl.ds(0, 31)], dst_ref=target.at[pl.ds(0, 31)],
            send_sem=go_sem.at[k], recv_sem=come_sem.at[k],
            device_id=(p, lax.rem(r + 1, rows)), device_id_type=MESH,
        )

    def tendency_copy(target):
        return pltpu.make_async_remote_copy(
            src_ref=rs.at[target], dst_ref=rt.at[r], send_sem=go_sem.at[2],
            recv_sem=come_sem.at[2], device_id=(p, target), device_id_type=MESH,
        )

    mine = lax.div(r, 2 * TILES)

    def finish(group, own):
        first = pl.multiple_of(group * TILES, TILES)
        near = ar.at[pl.ds(2 * first, 2 * TILES)]
        due = ar.at[pl.ds(2 * first, 2 * TILES - own)]
        pltpu.make_async_copy(due, due, tile_sem.at[group]).wait()
        near = 0.3 * near[...].reshape(8 * TILES, 128)
        parts = [part.astype(F32) for part in (*halves(near), *halves(pltpu.roll(near, 64, 1)))]
        near = jnp.concatenate(
            [parts[k][8 * t : 8 * t + 8] for t in range(TILES) for k in (0, 2, 1, 3)], axis=0
        ).T[0:64]
        near = [near] + [pltpu.roll(near, 128 - 32 * t, 1) for t in range(1, TILES)]
        pulled = dot(jnp.concatenate(near, axis=0).astype(BF16), spread[...])
        pulled = [
            [pulled[64 * t : 64 * t + 64, 128 * f : 128 * f + 128] for f in range(3)]
            for t in range(TILES)
        ]
        fields = []
        for t in range(TILES):
            one = [ys[first + t, 64 * f : 64 * f + 64, :] + pulled[t][f] for f in range(3)]
            one[0], one[1] = condensed(one[0], one[1], wt[first + t], saturation)
            fields.append(one)
        both = [jnp.concatenate(halves(value), axis=1) for one in fields for value in one]
        shifted = dot(jnp.concatenate(both, axis=0), along[...])
        change = []
        for t in range(TILES):
            at = pl.ds(pl.multiple_of(128 * (first + t), 128), 128)
            one = fields[t]
            momentum = -0.1 * one[2]
            two = []
            for f in range(3):
                line = 64 * (3 * t + f)
                moved = transported(one[f], shifted[line : line + 64], momentum)
                two.append(moved + pulled[t][f])
            two[0], two[1] = condensed(two[0], two[1], wt[first + t], saturation)
            parts = []
            for f in range(3):
                parts.append(halves(two[f]))
                ob[f, :, at] = parts[f][0][0:CRM_LEV]
            change += [jnp.concatenate([part[h] for part in parts], axis=1) for h in range(2)]
        mean = slot_means(means[...], jnp.concatenate(change, axis=0))
        for t in range(TILES):
            part = mean[:, 128 * t : 128 * t + 128]
            part = part + pltpu.roll(part, 64, 1)
            message = jnp.where(iota((8, 128), 1) < 64, part[0:8], part[8:16]) - xs[first + t]
            for pair in range(2):
                rs[2 * (first + t) + pair] = message[4 * pair : 4 * pair + 4]
        for k in range(2 * TILES):
            target = 2 * first + k
            if own:
                pl.when(target != r)(tendency_copy(target).start)
            else:
                tendency_copy(target).start()

    def others(k, carry):
        away = (1 - 2 * (k & 1)) * ((k + 2) >> 1)
        finish(lax.rem(mine + GROUPS + away, GROUPS), 0)
        return carry

    lax.fori_loop(0, GROUPS - 1, others, None)
    finish(mine, 1)
    rt[r] = rs[r]

    store = pltpu.make_async_copy(ob, crm_out, store_sem.at[0])
    store.start()

    loads[8].wait()
    for field in range(4):
        dh[:, 128 * field : 128 * field + LEV] = dot_split(table(0), xin[field])
    state_copies = []
    for slot in range(8):
        at = pl.ds(STATE_AT[slot], STATE_ROWS[slot])
        state_copies.append(
            pltpu.make_async_remote_copy(
                src_ref=dh.at[at], dst_ref=dr.at[at], send_sem=go_sem.at[1],
                recv_sem=come_sem.at[1], device_id=around[slot], device_id_type=MESH,
            )
        )
        state_copies[-1].start()

    loads[9].wait()
    lane, line = iota((32, 128), 1), iota((32, 128), 0)
    home = jnp.sum(
        jnp.where(lane == line, jnp.broadcast_to(position, (32, 128)), 0.0), axis=1, keepdims=True
    )
    code = (lane >> 2).astype(F32)
    match = jnp.concatenate(
        [jnp.where(home - s == 2.0 * code, 1.0, 0.0) for s in range(2)], axis=1
    )
    lane = iota((32, 256), 1)
    for field in range(3):
        place[32 * field : 32 * field + 32, :] = jnp.where((lane & 3) == field, match, 0.0).astype(BF16)
    match = match.astype(BF16)
    for h in range(2):
        for half, piece in enumerate(table(4 + h, HALO)):
            at = (2 * half + h) * HALO
            post[at : at + HALO, :] = (
                pick[...] * dot(piece[:, 0:32], match)
            ).astype(BF16)

    for field in range(4):
        od[field, :, 0:LEV] = dot_split(table(1), xin[field])

    all_of(rs, rt, 2).wait_recv()
    given = rt[...].reshape(128, 128)
    lane = iota((128, 128), 1)
    given = [jnp.where(lane < CRM_LEV, value, 0.0) for value in (given, pltpu.roll(given, 64, 1))]
    given = jnp.concatenate(halves(jnp.concatenate(given, axis=0)), axis=1)
    sent = dot(post[...], given)
    sent = [sent[HALO * k : HALO * k + HALO] for k in range(4)]
    sent = [sent[h][:, 0:128] + sent[h][:, 128:256] + sent[2 + h][:, 0:128] for h in range(2)]
    hs[...] = sent[0] + pltpu.roll(sent[1], 64, 1)
    for slot in (4, 5, 6, 7, 0, 1, 2, 3):
        at = pl.ds(CELL_AT[slot], CELL_ROWS[slot])
        pltpu.make_async_remote_copy(
            src_ref=hs.at[at], dst_ref=hr.at[at], send_sem=go_sem.at[3],
            recv_sem=come_sem.at[3], device_id=around[slot], device_id_type=MESH,
        ).start()
    cells = dot(place[...], given)
    cells = cells[:, 0:128] + cells[:, 128:256]
    own = table(3)
    own = own[0][:, 0:32], own[1][:, 0:32]
    for field in range(3):
        od[field, :, 0:LEV] += dot_split(own, cells[32 * field : 32 * field + 32])[:, 0:LEV]

    pltpu.make_async_remote_copy(
        src_ref=dh, dst_ref=dr, send_sem=go_sem.at[1], recv_sem=come_sem.at[1],
        device_id=around[0], device_id_type=MESH,
    ).wait_recv()
    for field in range(4):
        od[field, :, 0:LEV] += dot_split(table(2), dr[:, 128 * field : 128 * field + 128])[:, 0:LEV]

    halo_copy = pltpu.make_async_remote_copy(
        src_ref=hs, dst_ref=hr, send_sem=go_sem.at[3],
        recv_sem=come_sem.at[3], device_id=around[0], device_id_type=MESH,
    )
    part = pltpu.make_async_copy(od, part_out, store_sem.at[1])
    part.start()
    halo_copy.wait_recv()
    all_of(og, ar, 0).wait_send()
    all_of(rs, rt, 2).wait_send()
    pltpu.make_async_remote_copy(
        src_ref=dh, dst_ref=dr, send_sem=go_sem.at[1], recv_sem=come_sem.at[1],
        device_id=around[0], device_id_type=MESH,
    ).wait_send()
    halo_copy.wait_send()
    store.wait()
    part.wait()


def last_kernel(came_in, part, arrive, crm_in, dyn_out, crm_out, od, sem):
    crm = pltpu.make_async_copy(crm_in, crm_out, sem.at[0])
    crm.start()
    stores = [pltpu.make_async_copy(od.at[f], dyn_out.at[f], sem.at[1 + f]) for f in range(4)]
    od[3] = part[3, :, 0:LEV]
    stores[3].start()
    lane = iota((HALO, 128), 1)
    came = came_in[...]
    came = [jnp.where(lane < 64, value, 0.0) for value in (came, pltpu.roll(came, 64, 1))]
    came = jnp.concatenate(came + [jnp.zeros((256 - 2 * HALO, 128), F32)], axis=0)
    came = jnp.concatenate(halves(came), axis=1)
    taken = dot(arrive[...], came)
    for f in range(3):
        high, low = taken[128 * f : 128 * f + 128], taken[384 + 128 * f : 512 + 128 * f]
        od[f] = part[f, :, 0:LEV] + (high[:, 0:128] + high[:, 128:256] + low[:, 0:128])[:, 0:LEV]
        stores[f].start()
    crm.wait()
    for store in stores:
        store.wait()


def per_device(dyn_state, crm_state, cloud_mask, span_of):
    *consts, arrive = (jnp.asarray(value) for value in tables())
    vmem = pltpu.VMEM
    scratch = [
        vmem((4, 128, LEV), F32), vmem((3, CRM_LEV, 2048), BF16), vmem((CRM_LEV, 2048), jnp.int32),
        vmem((1, 32), jnp.int32),
    ]
    scratch += [vmem(value.shape, value.dtype) for value in consts]
    scratch += [
        vmem((8, 128), F32),
        vmem((16, 8, 128), F32), vmem((16, 192, 128), F32), vmem((16, 64, 128), F32),
        vmem((128, 128), F32),
        vmem((32, 4, 128), F32), vmem((32, 4, 128), F32),
        vmem((32, 4, 128), F32), vmem((32, 4, 128), F32),
        vmem((128, 512), F32), vmem((128, 512), F32),
        vmem((HALO, 128), F32),
        vmem((3, CRM_LEV, 2048), BF16), vmem((4, 128, 128), F32),
        vmem((96, 256), BF16), vmem((4 * HALO, 256), BF16),
        pltpu.SemaphoreType.DMA((10,)), pltpu.SemaphoreType.DMA((2,)),
        pltpu.SemaphoreType.DMA((4,)), pltpu.SemaphoreType.DMA((4,)), pltpu.SemaphoreType.DMA((GROUPS,)),
    ]
    nodes = dyn_state.transpose(0, 2, 3, 1).reshape(4, 128, LEV)
    operands = (nodes, crm_state, cloud_mask, span_of.T, *consts)
    anywhere = pl.BlockSpec(memory_space=pl.ANY)
    came, part, crm = pl.pallas_call(
        kernel,
        out_shape=(
            vmem((HALO, 128), F32), vmem((4, 128, 128), F32), vmem((3, CRM_LEV, 2048), BF16)
        ),
        in_specs=[anywhere] * 10,
        out_specs=[anywhere] * 3,
        scratch_shapes=scratch,
        compiler_params=pltpu.CompilerParams(
            collective_id=0, has_side_effects=True, vmem_limit_bytes=40 * 2**20
        ),
        name="physics_step",
    )(*(pltpu.with_memory_space_constraint(value, pltpu.HBM) for value in operands))
    near = pl.BlockSpec(memory_space=pltpu.VMEM)
    dyn, crm = pl.pallas_call(
        last_kernel,
        out_shape=(
            pltpu.HBM((4, 128, LEV), F32), pltpu.HBM((3, CRM_LEV, 2048), BF16)
        ),
        in_specs=[near, near, near, anywhere],
        out_specs=[anywhere] * 2,
        scratch_shapes=[
            vmem((4, 128, LEV), F32), pltpu.SemaphoreType.DMA((5,))
        ],
        compiler_params=pltpu.CompilerParams(vmem_limit_bytes=8 * 2**20),
        name="last_step",
    )(came, part, arrive, crm)
    return dyn.reshape(4, 16, 8, LEV).transpose(0, 3, 1, 2), crm


def solution(mesh):
    return jax.shard_map(
        per_device,
        mesh=mesh,
        in_specs=(
            P(None, None, "blk", "row"),
            P(None, None, ("blk", "row")),
            P(None, ("blk", "row")),
            P(("blk", "row"), None),
        ),
        out_specs=(P(None, None, "blk", "row"), P(None, None, ("blk", "row"))),
        check_vma=False,
    )
```

```python
import functools

import jax
import jax.numpy as jnp
import numpy as np
from jax import lax
from jax.experimental import pallas as pl
from jax.experimental.pallas import tpu as pltpu
from jax.sharding import PartitionSpec as P

MESH = pl.DeviceIdType.MESH
LEV, CRM_LEV, CRM_COLS = 72, 58, 32
F32, BF16 = jnp.float32, jnp.bfloat16
SLOTS = ((0, -1), (0, 1), (-1, 0), (1, 0), (-1, -1), (-1, 1), (1, -1), (1, 1))
STATE_ROWS = (32, 32, 16, 16, 8, 8, 8, 8)
TILES, GROUPS = 4, 4
CELL_RANK = (16, 16, 8, 8, 2, 2, 2, 2)
CELL_ROWS = (24, 24, 16, 16, 8, 8, 8, 8)
STATE_AT = tuple(int(v) for v in np.cumsum((0,) + STATE_ROWS))
CELL_AT = tuple(int(v) for v in np.cumsum((0,) + CELL_ROWS))
HALO = CELL_AT[-1]


def poly_times(first_poly, second_poly):
    product = [0.0] * (len(first_poly) + len(second_poly) - 1)
    for i, first in enumerate(first_poly):
        for j, second in enumerate(second_poly):
            product[i + j] += first * second
    return product


def poly_slope(coeffs, point):
    return sum(power * coeffs[power] * point ** (power - 1) for power in range(1, len(coeffs)))


def poly_integral(coeffs, low, high):
    return sum(
        coeffs[power] * (high ** (power + 1) - low ** (power + 1)) / (power + 1)
        for power in range(len(coeffs))
    )


def element_tables():
    root_five = float(np.sqrt(5.0))
    gll_nodes = [-1.0, -1.0 / root_five, 1.0 / root_five, 1.0]
    weights = np.array([1.0 / 6.0, 5.0 / 6.0, 5.0 / 6.0, 1.0 / 6.0])
    derivative = np.zeros((4, 4))
    to_cells = np.zeros((2, 4))
    for basis in range(4):
        coeffs = [1.0]
        for other in range(4):
            if other != basis:
                denominator = gll_nodes[basis] - gll_nodes[other]
                coeffs = poly_times(coeffs, [-gll_nodes[other] / denominator, 1.0 / denominator])
        for node in range(4):
            derivative[node, basis] = poly_slope(coeffs, gll_nodes[node])
        to_cells[0, basis] = poly_integral(coeffs, -1.0, 0.0)
        to_cells[1, basis] = poly_integral(coeffs, 0.0, 1.0)
    to_nodes = np.array([[1.0, 0.0], [1.0, 0.0], [0.0, 1.0], [0.0, 1.0]])
    edge_weights = np.array([1.0 / 3.0, 5.0 / 6.0, 5.0 / 6.0, 1.0 / 3.0])
    return derivative, weights, to_cells, to_nodes, edge_weights


def line_operators(elements):
    derivative, weights, _, _, edge_weights = element_tables()
    count = elements * 4 * 3
    weight = np.tile(weights, elements * 3)
    fold = np.eye(count)
    for node in range(count):
        if node % 4 == 0:
            fold[node, (node - 1) % count] += 1.0
        if node % 4 == 3:
            fold[node, (node + 1) % count] += 1.0
    fold = fold / np.tile(edge_weights, elements * 3)[:, None]
    smooth = fold * weight
    stiff = np.kron(np.eye(elements * 3), derivative.T @ np.diag(weights) @ derivative)
    mine = slice(elements * 4, elements * 8)
    return smooth[mine], (fold @ stiff @ smooth)[mine], (smooth @ smooth)[mine]


def split(value):
    high = np.asarray(value, np.float32).astype(jnp.bfloat16)
    return high, (np.asarray(value, np.float32) - high.astype(np.float32)).astype(jnp.bfloat16)


@functools.cache
def tables():
    _, _, to_cells, to_nodes, _ = element_tables()
    smooth_x, stiff_x, mass_x = line_operators(4)
    smooth_y, stiff_y, mass_y = line_operators(2)
    nodes = np.kron(np.kron(np.eye(4), to_nodes), np.kron(np.eye(2), to_nodes))

    def block(dx, dy):
        x, y = slice(16 * (dx + 1), 16 * (dx + 2)), slice(8 * (dy + 1), 8 * (dy + 2))
        return np.kron(smooth_x[:, x], smooth_y[:, y]) - 0.01 * (
            np.kron(stiff_x[:, x], mass_y[:, y]) + np.kron(mass_x[:, x], stiff_y[:, y])
        )

    cell_sums = np.zeros((32, 128))
    cell_sums[:] = np.kron(np.kron(np.eye(4), to_cells), np.kron(np.eye(2), to_cells))
    mine = block(0, 0)
    own = np.zeros((128, 128))
    own[:, :32] = mine @ nodes
    outer, inner = np.zeros((128, 128)), np.zeros((128, 128))
    arrive = np.zeros((3, 128, 256))
    leave = np.zeros((2, HALO, 128))
    pick = np.zeros((HALO, 256), np.float32)
    for slot, (dx, dy) in enumerate(SLOTS):
        part = block(dx, dy)
        left, scale, right = np.linalg.svd(part)
        rank = int((scale > 1e-10).sum())
        assert rank <= STATE_ROWS[slot]
        at = STATE_AT[slot]
        outer[:, at : at + rank] = left[:, :rank] * np.sqrt(scale[:rank])
        inner[at : at + rank] = right[:rank] * np.sqrt(scale[:rank])[:, None]
        left, scale, right = np.linalg.svd(part @ nodes, full_matrices=False)
        rank = int((scale > 1e-10).sum())
        assert rank <= CELL_RANK[slot]
        left, right = left * np.sqrt(scale), right * np.sqrt(scale)[:, None]
        half = CELL_RANK[slot] // 2
        for field in range(3):
            at = CELL_AT[slot] + field * half
            pick[at : at + half, field::4] = 1.0
            for h in range(2):
                leave[h, at : at + half, :32] = right[h : 2 * half : 2]
                arrive[field, :, h * HALO + at : h * HALO + at + half] = left[:, h : 2 * half : 2]
    pieces = []
    for matrix in (inner, mine, outer, own, leave[0], leave[1]):
        pieces.extend(split(matrix))
    matrices = np.concatenate(pieces, axis=0)
    cell_sums = np.concatenate(split(cell_sums), axis=0)
    arrive = np.concatenate(split(arrive.reshape(384, 256)), axis=0)

    cell = np.arange(128)
    same = (cell[:, None] // 32) == (cell[None, :] // 32)
    step = (cell[:, None] - cell[None, :]) % 32
    east, west = same & (step == 1), same & (step == 31)
    along = np.concatenate([1.0 * east + 1.0 * west - same / 16.0, 1.0 * east - 1.0 * west], axis=1)
    along = np.concatenate([along, along], axis=0).astype(jnp.bfloat16)

    spread = np.zeros((16, 384))
    for s in range(2):
        for pair in range(2):
            for field in range(3):
                at = field * 128 + pair * 64 + s * 32
                spread[s * 8 + pair * 4 + field, at : at + 32] = 1.0
    means = (spread / 32.0).astype(jnp.bfloat16)
    spread = np.concatenate([spread, spread, np.zeros((96, 384))], axis=0).astype(jnp.bfloat16)
    return cell_sums, matrices, along, spread, means, pick, arrive


def halves(value):
    high = value.astype(BF16)
    return high, (value - high.astype(F32)).astype(BF16)


def dot(left, right):
    return jnp.dot(left, right, preferred_element_type=F32)


def dot_split(left, right):
    high, low = halves(right)
    return dot(left[0], high) + dot(left[1], high) + dot(left[0], low)


def slot_means(weights, fields):
    return lax.dot_general(
        weights, fields, (((1,), (1,)), ((), ())), preferred_element_type=F32
    )


def iota(shape, axis):
    return lax.broadcasted_iota(jnp.int32, shape, axis)


def levels_moved(field):
    sub = iota((8, 128), 0)
    rows = [field[8 * k : 8 * k + 8] for k in range(8)]
    up = [pltpu.roll(value, 7, 0) for value in rows]
    down = [pltpu.roll(value, 1, 0) for value in rows]
    moved = []
    for k in range(8):
        above = jnp.where(sub == 7, up[k + 1], up[k]) if k < 7 else jnp.where(sub >= 1, rows[7], up[7])
        below = jnp.where(sub == 0, down[k - 1] if k else rows[0], down[k])
        moved.append(above + below)
    return jnp.concatenate(moved, axis=0)


def transported(field, along, momentum):
    return (
        0.4 * field
        + 0.15 * (along[:, :128] + levels_moved(field))
        + momentum * along[:, 128:]
    )


def condensed(heat, water, wet, saturation):
    cond = wet * jnp.maximum(water - 0.5 * heat - saturation, 0.0)
    return heat + 0.8 * cond, water - cond


def kernel(
    dyn, crm, mask, span, sums_in, matrices, along_in, spread_in, means_in, pick_in,
    hr, part_out, crm_out,
    xin, xb, mk, sp, sums, mat, along, spread, means, pick,
    spans, xs, ys, wt, cat, og, ar, rs, rt, dh, dr, hs, ob, od, place, post,
    load_sem, store_sem, go_sem, come_sem, tile_sem,
):
    p, r = lax.axis_index("blk"), lax.axis_index("row")
    rows, blocks = lax.axis_size("row"), lax.axis_size("blk")
    barrier = pltpu.get_barrier_semaphore()

    def far_first(k):
        return lax.rem(r + 16 + (1 - 2 * (k & 1)) * ((k + 1) >> 1), rows)

    def greet(k, carry):
        pl.semaphore_signal(barrier, inc=1, device_id=(p, far_first(k)), device_id_type=MESH)
        return carry

    lax.fori_loop(0, rows - 1, greet, None, unroll=True)
    around = [
        (lax.rem(p + blocks - dx, blocks), lax.rem(r + rows - dy, rows)) for dx, dy in SLOTS
    ]
    for slot in range(2, 8):
        pl.semaphore_signal(barrier, inc=1, device_id=around[slot], device_id_type=MESH)

    loads = [
        pltpu.make_async_copy(source, target, load_sem.at[k])
        for k, (source, target) in enumerate(
            ((span, sp), (sums_in, sums), (dyn, xin), (crm, xb), (mask, mk), (along_in, along),
             (spread_in, spread), (means_in, means), (matrices, mat), (pick_in, pick))
        )
    ]
    for load in loads[:3]:
        load.start()

    cat[...] = jnp.zeros_like(cat)
    spans[...] = jnp.zeros_like(spans)

    def table(k, lines=128):
        at = (0, 256, 512, 768, 1024, 1024 + 2 * HALO)[k]
        return mat[at : at + lines], mat[at + lines : at + 2 * lines]

    loads[0].wait()
    spans[0:1, 0:32] = sp[...].astype(F32)
    named = spans[...]
    named = named + pltpu.roll(named, 32, 1)
    named = named + pltpu.roll(named, 64, 1)
    lane, line = iota((32, 128), 1), iota((32, 128), 0)
    across = jnp.broadcast_to(named[0:1, :], (32, 128))
    down = jnp.sum(jnp.where(lane == line, across, 0.0), axis=1, keepdims=True)
    earlier = jnp.where((down == across) & (line < (lane & 31)), 1.0, 0.0)
    position = 2.0 * named[0:1, :] + jnp.sum(earlier, axis=0, keepdims=True)
    lane, line = iota((128, 128), 1), iota((128, 128), 0)
    wanted = (2 * line - (line & 3)).astype(F32)
    offered = 4.0 * jnp.broadcast_to(position, (128, 128)) + (lane >> 5).astype(F32)
    send_to = jnp.concatenate(
        [jnp.where(offered - 4.0 * s == wanted, 1.0, 0.0) for s in range(2)], axis=1
    ).astype(BF16)

    loads[1].wait()
    loads[2].wait()
    for load in loads[3:6]:
        load.start()
    for field in range(3):
        cat[32 * field : 32 * field + 32, 0:LEV] = dot_split((sums[0:32], sums[32:64]), xin[field])
    first = jnp.where(lane < CRM_LEV, cat[...], 0.0)
    high, low = halves(jnp.concatenate([first, pltpu.roll(first, 64, 1)], axis=0))
    sent = dot(send_to, jnp.concatenate([high, low], axis=1))
    og[...] = (sent[:, :128] + sent[:, 128:]).reshape(32, 4, 128)

    pl.semaphore_wait(barrier, rows - 1 + 6)

    def profile_copy(target):
        return pltpu.make_async_remote_copy(
            src_ref=og.at[target], dst_ref=ar.at[r], send_sem=go_sem.at[0],
            recv_sem=tile_sem.at[lax.div(r, 2 * TILES)], device_id=(p, target), device_id_type=MESH,
        )

    def send_profile(k, carry):
        profile_copy(far_first(k)).start()
        return carry

    lax.fori_loop(0, rows - 1, send_profile, None, unroll=True)
    ar[r] = og[r]

    for load in loads[6:]:
        load.start()

    for k in range(3, 6):
        loads[k].wait()
    row = iota((64, 128), 0)
    saturation = 0.5 - row.astype(F32) / CRM_LEV
    rest = jnp.zeros((64 - CRM_LEV, 128), F32)

    def begin(group, carry):
        first = pl.multiple_of(group * TILES, TILES)
        state = []
        for t in range(TILES):
            at = pl.ds(pl.multiple_of(128 * (first + t), 128), 128)
            wt[first + t] = jnp.concatenate([0.5 * mk[:, at].astype(F32), rest], axis=0)
            for f in range(3):
                state.append(jnp.concatenate([xb[f, :, at].astype(F32), rest], axis=0))
        shifted = dot(jnp.concatenate(state, axis=0).astype(BF16), along[0:128, :])
        for t in range(TILES):
            momentum = -0.1 * state[3 * t + 2]
            for f in range(3):
                line = 64 * (3 * t + f)
                moved = transported(state[3 * t + f], shifted[line : line + 64], momentum)
                ys[first + t, 64 * f : 64 * f + 64, :] = moved
        start = jnp.concatenate(
            [jnp.concatenate(state[3 * t : 3 * t + 3], axis=1) for t in range(TILES)], axis=0
        )
        mean = slot_means(means[...], start.astype(BF16))
        for t in range(TILES):
            part = mean[:, 64 * t : 64 * t + 64]
            xs[first + t] = jnp.concatenate([part[0:8], part[8:16]], axis=1)
        return carry

    loads[7].wait()
    lax.fori_loop(0, GROUPS, begin, None)
    loads[6].wait()

    def all_of(source, target, k):
        return pltpu.make_async_remote_copy(
            src_ref=source.at[pl.ds(0, 31)], dst_ref=target.at[pl.ds(0, 31)],
            send_sem=go_sem.at[k], recv_sem=come_sem.at[k],
            device_id=(p, lax.rem(r + 1, rows)), device_id_type=MESH,
        )

    def tendency_copy(target):
        return pltpu.make_async_remote_copy(
            src_ref=rs.at[target], dst_ref=rt.at[r], send_sem=go_sem.at[2],
            recv_sem=come_sem.at[2], device_id=(p, target), device_id_type=MESH,
        )

    mine = lax.div(r, 2 * TILES)

    def finish(k, carry):
        late = k >> 1
        group = (3 - k) * (1 - late) + (k - 2) * late
        first = pl.multiple_of(group * TILES, TILES)
        near = ar.at[pl.ds(2 * first, 2 * TILES)]

        def wait(count):
            due = ar.at[pl.ds(2 * first, count)]
            pltpu.make_async_copy(due, due, tile_sem.at[group]).wait()

        pl.when(group != mine)(lambda: wait(2 * TILES))
        pl.when(group == mine)(lambda: wait(2 * TILES - 1))
        near = 0.3 * near[...].reshape(8 * TILES, 128)
        parts = [part.astype(F32) for part in (*halves(near), *halves(pltpu.roll(near, 64, 1)))]
        near = jnp.concatenate(
            [parts[k][8 * t : 8 * t + 8] for t in range(TILES) for k in (0, 2, 1, 3)], axis=0
        ).T[0:64]
        near = [near] + [pltpu.roll(near, 128 - 32 * t, 1) for t in range(1, TILES)]
        pulled = dot(jnp.concatenate(near, axis=0).astype(BF16), spread[...])
        pulled = [
            [pulled[64 * t : 64 * t + 64, 128 * f : 128 * f + 128] for f in range(3)]
            for t in range(TILES)
        ]
        fields = []
        for t in range(TILES):
            one = [ys[first + t, 64 * f : 64 * f + 64, :] + pulled[t][f] for f in range(3)]
            one[0], one[1] = condensed(one[0], one[1], wt[first + t], saturation)
            fields.append(one)
        both = [jnp.concatenate(halves(value), axis=1) for one in fields for value in one]
        shifted = dot(jnp.concatenate(both, axis=0), along[...])
        change = []
        for t in range(TILES):
            at = pl.ds(pl.multiple_of(128 * (first + t), 128), 128)
            one = fields[t]
            momentum = -0.1 * one[2]
            two = []
            for f in range(3):
                line = 64 * (3 * t + f)
                moved = transported(one[f], shifted[line : line + 64], momentum)
                two.append(moved + pulled[t][f])
            two[0], two[1] = condensed(two[0], two[1], wt[first + t], saturation)
            parts = []
            for f in range(3):
                parts.append(halves(two[f]))
                ob[f, :, at] = parts[f][0][0:CRM_LEV]
            change += [jnp.concatenate([part[h] for part in parts], axis=1) for h in range(2)]
        mean = [
            slot_means(means[...], jnp.concatenate(change[2 * t : 2 * t + 2], axis=0))
            for t in range(TILES)
        ]
        for t in range(TILES):
            part = mean[t] + pltpu.roll(mean[t], 64, 1)
            message = jnp.where(iota((8, 128), 1) < 64, part[0:8], part[8:16]) - xs[first + t]
            for pair in range(2):
                rs[2 * (first + t) + pair] = message[4 * pair : 4 * pair + 4]
        for k in range(2 * TILES):
            target = 2 * first + k
            pl.when(target != r)(tendency_copy(target).start)
        return carry

    lax.fori_loop(0, GROUPS, finish, None)
    rt[r] = rs[r]

    store = pltpu.make_async_copy(ob, crm_out, store_sem.at[0])
    store.start()

    loads[8].wait()
    for field in range(4):
        dh[:, 128 * field : 128 * field + LEV] = dot_split(table(0), xin[field])
    state_copies = []
    for slot in range(8):
        at = pl.ds(STATE_AT[slot], STATE_ROWS[slot])
        state_copies.append(
            pltpu.make_async_remote_copy(
                src_ref=dh.at[at], dst_ref=dr.at[at], send_sem=go_sem.at[1],
                recv_sem=come_sem.at[1], device_id=around[slot], device_id_type=MESH,
            )
        )
        state_copies[-1].start()

    loads[9].wait()
    lane, line = iota((32, 128), 1), iota((32, 128), 0)
    home = jnp.sum(
        jnp.where(lane == line, jnp.broadcast_to(position, (32, 128)), 0.0), axis=1, keepdims=True
    )
    code = (lane >> 2).astype(F32)
    match = jnp.concatenate(
        [jnp.where(home - s == 2.0 * code, 1.0, 0.0) for s in range(2)], axis=1
    )
    lane = iota((32, 256), 1)
    for field in range(3):
        place[32 * field : 32 * field + 32, :] = jnp.where((lane & 3) == field, match, 0.0).astype(BF16)
    match = match.astype(BF16)
    for h in range(2):
        for half, piece in enumerate(table(4 + h, HALO)):
            at = (2 * half + h) * HALO
            post[at : at + HALO, :] = (
                pick[...] * dot(piece[:, 0:32], match)
            ).astype(BF16)

    for field in range(4):
        od[field, :, 0:LEV] = dot_split(table(1), xin[field])

    all_of(rs, rt, 2).wait_recv()
    given = rt[...].reshape(128, 128)
    lane = iota((128, 128), 1)
    given = [jnp.where(lane < CRM_LEV, value, 0.0) for value in (given, pltpu.roll(given, 64, 1))]
    given = jnp.concatenate(halves(jnp.concatenate(given, axis=0)), axis=1)
    sent = dot(post[...], given)
    sent = [sent[HALO * k : HALO * k + HALO] for k in range(4)]
    sent = [sent[h][:, 0:128] + sent[h][:, 128:256] + sent[2 + h][:, 0:128] for h in range(2)]
    hs[...] = sent[0] + pltpu.roll(sent[1], 64, 1)
    for slot in (4, 5, 6, 7, 0, 1, 2, 3):
        at = pl.ds(CELL_AT[slot], CELL_ROWS[slot])
        pltpu.make_async_remote_copy(
            src_ref=hs.at[at], dst_ref=hr.at[at], send_sem=go_sem.at[3],
            recv_sem=come_sem.at[3], device_id=around[slot], device_id_type=MESH,
        ).start()
    cells = dot(place[...], given)
    cells = cells[:, 0:128] + cells[:, 128:256]
    own = table(3)
    own = own[0][:, 0:32], own[1][:, 0:32]
    for field in range(3):
        od[field, :, 0:LEV] += dot_split(own, cells[32 * field : 32 * field + 32])[:, 0:LEV]

    pltpu.make_async_remote_copy(
        src_ref=dh, dst_ref=dr, send_sem=go_sem.at[1], recv_sem=come_sem.at[1],
        device_id=around[0], device_id_type=MESH,
    ).wait_recv()
    for field in range(4):
        od[field, :, 0:LEV] += dot_split(table(2), dr[:, 128 * field : 128 * field + 128])[:, 0:LEV]

    halo_copy = pltpu.make_async_remote_copy(
        src_ref=hs, dst_ref=hr, send_sem=go_sem.at[3],
        recv_sem=come_sem.at[3], device_id=around[0], device_id_type=MESH,
    )
    part = pltpu.make_async_copy(od, part_out, store_sem.at[1])
    part.start()
    halo_copy.wait_recv()
    all_of(og, ar, 0).wait_send()
    all_of(rs, rt, 2).wait_send()
    pltpu.make_async_remote_copy(
        src_ref=dh, dst_ref=dr, send_sem=go_sem.at[1], recv_sem=come_sem.at[1],
        device_id=around[0], device_id_type=MESH,
    ).wait_send()
    halo_copy.wait_send()
    store.wait()
    part.wait()


def last_kernel(came_in, part, arrive, crm_in, dyn_out, crm_out, od, sem):
    crm = pltpu.make_async_copy(crm_in, crm_out, sem.at[0])
    crm.start()
    stores = [pltpu.make_async_copy(od.at[f], dyn_out.at[f], sem.at[1 + f]) for f in range(4)]
    od[3] = part[3, :, 0:LEV]
    stores[3].start()
    lane = iota((HALO, 128), 1)
    came = came_in[...]
    came = [jnp.where(lane < 64, value, 0.0) for value in (came, pltpu.roll(came, 64, 1))]
    came = jnp.concatenate(came + [jnp.zeros((256 - 2 * HALO, 128), F32)], axis=0)
    came = jnp.concatenate(halves(came), axis=1)
    taken = dot(arrive[...], came)
    for f in range(3):
        high, low = taken[128 * f : 128 * f + 128], taken[384 + 128 * f : 512 + 128 * f]
        od[f] = part[f, :, 0:LEV] + (high[:, 0:128] + high[:, 128:256] + low[:, 0:128])[:, 0:LEV]
        stores[f].start()
    crm.wait()
    for store in stores:
        store.wait()


def per_device(dyn_state, crm_state, cloud_mask, span_of):
    *consts, arrive = (jnp.asarray(value) for value in tables())
    vmem = pltpu.VMEM
    scratch = [
        vmem((4, 128, LEV), F32), vmem((3, CRM_LEV, 2048), BF16), vmem((CRM_LEV, 2048), jnp.int32),
        vmem((1, 32), jnp.int32),
    ]
    scratch += [vmem(value.shape, value.dtype) for value in consts]
    scratch += [
        vmem((8, 128), F32),
        vmem((16, 8, 128), F32), vmem((16, 192, 128), F32), vmem((16, 64, 128), F32),
        vmem((128, 128), F32),
        vmem((32, 4, 128), F32), vmem((32, 4, 128), F32),
        vmem((32, 4, 128), F32), vmem((32, 4, 128), F32),
        vmem((128, 512), F32), vmem((128, 512), F32),
        vmem((HALO, 128), F32),
        vmem((3, CRM_LEV, 2048), BF16), vmem((4, 128, 128), F32),
        vmem((96, 256), BF16), vmem((4 * HALO, 256), BF16),
        pltpu.SemaphoreType.DMA((10,)), pltpu.SemaphoreType.DMA((2,)),
        pltpu.SemaphoreType.DMA((4,)), pltpu.SemaphoreType.DMA((4,)), pltpu.SemaphoreType.DMA((GROUPS,)),
    ]
    nodes = dyn_state.transpose(0, 2, 3, 1).reshape(4, 128, LEV)
    operands = (nodes, crm_state, cloud_mask, span_of.T, *consts)
    anywhere = pl.BlockSpec(memory_space=pl.ANY)
    came, part, crm = pl.pallas_call(
        kernel,
        out_shape=(
            vmem((HALO, 128), F32), vmem((4, 128, 128), F32), vmem((3, CRM_LEV, 2048), BF16)
        ),
        in_specs=[anywhere] * 10,
        out_specs=[anywhere] * 3,
        scratch_shapes=scratch,
        compiler_params=pltpu.CompilerParams(
            collective_id=0, has_side_effects=True, vmem_limit_bytes=40 * 2**20
        ),
        name="physics_step",
    )(*(pltpu.with_memory_space_constraint(value, pltpu.HBM) for value in operands))
    near = pl.BlockSpec(memory_space=pltpu.VMEM)
    dyn, crm = pl.pallas_call(
        last_kernel,
        out_shape=(
            pltpu.HBM((4, 128, LEV), F32), pltpu.HBM((3, CRM_LEV, 2048), BF16)
        ),
        in_specs=[near, near, near, anywhere],
        out_specs=[anywhere] * 2,
        scratch_shapes=[
            vmem((4, 128, LEV), F32), pltpu.SemaphoreType.DMA((5,))
        ],
        compiler_params=pltpu.CompilerParams(vmem_limit_bytes=8 * 2**20),
        name="last_step",
    )(came, part, arrive, crm)
    return dyn.reshape(4, 16, 8, LEV).transpose(0, 3, 1, 2), crm


def solution(mesh):
    return jax.shard_map(
        per_device,
        mesh=mesh,
        in_specs=(
            P(None, None, "blk", "row"),
            P(None, None, ("blk", "row")),
            P(None, ("blk", "row")),
            P(("blk", "row"), None),
        ),
        out_specs=(P(None, None, "blk", "row"), P(None, None, ("blk", "row"))),
        check_vma=False,
    )
```

```python
import functools

import jax
import jax.numpy as jnp
import numpy as np
from jax import lax
from jax.experimental import pallas as pl
from jax.experimental.pallas import tpu as pltpu
from jax.sharding import PartitionSpec as P

MESH = pl.DeviceIdType.MESH
LEV, CRM_LEV, CRM_COLS = 72, 58, 32
F32, BF16 = jnp.float32, jnp.bfloat16
SLOTS = ((0, -1), (0, 1), (-1, 0), (1, 0), (-1, -1), (-1, 1), (1, -1), (1, 1))
STATE_ROWS = (32, 32, 16, 16, 8, 8, 8, 8)
TILES, GROUPS = 4, 4
CELL_RANK = (16, 16, 8, 8, 2, 2, 2, 2)
CELL_ROWS = (24, 24, 16, 16, 8, 8, 8, 8)
STATE_AT = tuple(int(v) for v in np.cumsum((0,) + STATE_ROWS))
CELL_AT = tuple(int(v) for v in np.cumsum((0,) + CELL_ROWS))
HALO = CELL_AT[-1]


def poly_times(first_poly, second_poly):
    product = [0.0] * (len(first_poly) + len(second_poly) - 1)
    for i, first in enumerate(first_poly):
        for j, second in enumerate(second_poly):
            product[i + j] += first * second
    return product


def poly_slope(coeffs, point):
    return sum(power * coeffs[power] * point ** (power - 1) for power in range(1, len(coeffs)))


def poly_integral(coeffs, low, high):
    return sum(
        coeffs[power] * (high ** (power + 1) - low ** (power + 1)) / (power + 1)
        for power in range(len(coeffs))
    )


def element_tables():
    root_five = float(np.sqrt(5.0))
    gll_nodes = [-1.0, -1.0 / root_five, 1.0 / root_five, 1.0]
    weights = np.array([1.0 / 6.0, 5.0 / 6.0, 5.0 / 6.0, 1.0 / 6.0])
    derivative = np.zeros((4, 4))
    to_cells = np.zeros((2, 4))
    for basis in range(4):
        coeffs = [1.0]
        for other in range(4):
            if other != basis:
                denominator = gll_nodes[basis] - gll_nodes[other]
                coeffs = poly_times(coeffs, [-gll_nodes[other] / denominator, 1.0 / denominator])
        for node in range(4):
            derivative[node, basis] = poly_slope(coeffs, gll_nodes[node])
        to_cells[0, basis] = poly_integral(coeffs, -1.0, 0.0)
        to_cells[1, basis] = poly_integral(coeffs, 0.0, 1.0)
    to_nodes = np.array([[1.0, 0.0], [1.0, 0.0], [0.0, 1.0], [0.0, 1.0]])
    edge_weights = np.array([1.0 / 3.0, 5.0 / 6.0, 5.0 / 6.0, 1.0 / 3.0])
    return derivative, weights, to_cells, to_nodes, edge_weights


def line_operators(elements):
    derivative, weights, _, _, edge_weights = element_tables()
    count = elements * 4 * 3
    weight = np.tile(weights, elements * 3)
    fold = np.eye(count)
    for node in range(count):
        if node % 4 == 0:
            fold[node, (node - 1) % count] += 1.0
        if node % 4 == 3:
            fold[node, (node + 1) % count] += 1.0
    fold = fold / np.tile(edge_weights, elements * 3)[:, None]
    smooth = fold * weight
    stiff = np.kron(np.eye(elements * 3), derivative.T @ np.diag(weights) @ derivative)
    mine = slice(elements * 4, elements * 8)
    return smooth[mine], (fold @ stiff @ smooth)[mine], (smooth @ smooth)[mine]


def split(value):
    high = np.asarray(value, np.float32).astype(jnp.bfloat16)
    return high, (np.asarray(value, np.float32) - high.astype(np.float32)).astype(jnp.bfloat16)


@functools.cache
def tables():
    _, _, to_cells, to_nodes, _ = element_tables()
    smooth_x, stiff_x, mass_x = line_operators(4)
    smooth_y, stiff_y, mass_y = line_operators(2)
    nodes = np.kron(np.kron(np.eye(4), to_nodes), np.kron(np.eye(2), to_nodes))

    def block(dx, dy):
        x, y = slice(16 * (dx + 1), 16 * (dx + 2)), slice(8 * (dy + 1), 8 * (dy + 2))
        return np.kron(smooth_x[:, x], smooth_y[:, y]) - 0.01 * (
            np.kron(stiff_x[:, x], mass_y[:, y]) + np.kron(mass_x[:, x], stiff_y[:, y])
        )

    cell_sums = np.zeros((32, 128))
    cell_sums[:] = np.kron(np.kron(np.eye(4), to_cells), np.kron(np.eye(2), to_cells))
    mine = block(0, 0)
    own = np.zeros((128, 128))
    own[:, :32] = mine @ nodes
    outer, inner = np.zeros((128, 128)), np.zeros((128, 128))
    arrive = np.zeros((3, 128, 256))
    leave = np.zeros((2, HALO, 128))
    pick = np.zeros((HALO, 256), np.float32)
    for slot, (dx, dy) in enumerate(SLOTS):
        part = block(dx, dy)
        left, scale, right = np.linalg.svd(part)
        rank = int((scale > 1e-10).sum())
        assert rank <= STATE_ROWS[slot]
        at = STATE_AT[slot]
        outer[:, at : at + rank] = left[:, :rank] * np.sqrt(scale[:rank])
        inner[at : at + rank] = right[:rank] * np.sqrt(scale[:rank])[:, None]
        left, scale, right = np.linalg.svd(part @ nodes, full_matrices=False)
        rank = int((scale > 1e-10).sum())
        assert rank <= CELL_RANK[slot]
        left, right = left * np.sqrt(scale), right * np.sqrt(scale)[:, None]
        half = CELL_RANK[slot] // 2
        for field in range(3):
            at = CELL_AT[slot] + field * half
            pick[at : at + half, field::4] = 1.0
            for h in range(2):
                leave[h, at : at + half, :32] = right[h : 2 * half : 2]
                arrive[field, :, h * HALO + at : h * HALO + at + half] = left[:, h : 2 * half : 2]
    pieces = []
    for matrix in (inner, mine, outer, own, leave[0], leave[1]):
        pieces.extend(split(matrix))
    matrices = np.concatenate(pieces, axis=0)
    cell_sums = np.concatenate(split(cell_sums), axis=0)
    arrive = np.concatenate(split(arrive.reshape(384, 256)), axis=0)

    cell = np.arange(128)
    same = (cell[:, None] // 32) == (cell[None, :] // 32)
    step = (cell[:, None] - cell[None, :]) % 32
    east, west = same & (step == 1), same & (step == 31)
    along = np.concatenate([1.0 * east + 1.0 * west - same / 16.0, 1.0 * east - 1.0 * west], axis=1)
    along = np.concatenate([along, along], axis=0).astype(jnp.bfloat16)

    spread = np.zeros((16, 384))
    for s in range(2):
        for pair in range(2):
            for field in range(3):
                at = field * 128 + pair * 64 + s * 32
                spread[s * 8 + pair * 4 + field, at : at + 32] = 1.0
    means = (spread / 32.0).astype(jnp.bfloat16)
    spread = np.concatenate([spread, spread, np.zeros((96, 384))], axis=0).astype(jnp.bfloat16)
    return cell_sums, matrices, along, spread, means, pick, arrive


def halves(value):
    high = value.astype(BF16)
    return high, (value - high.astype(F32)).astype(BF16)


def dot(left, right):
    return jnp.dot(left, right, preferred_element_type=F32)


def dot_split(left, right):
    high, low = halves(right)
    return dot(left[0], high) + dot(left[1], high) + dot(left[0], low)


def slot_means(weights, fields):
    return lax.dot_general(
        weights, fields, (((1,), (1,)), ((), ())), preferred_element_type=F32
    )


def iota(shape, axis):
    return lax.broadcasted_iota(jnp.int32, shape, axis)


def levels_moved(field):
    sub = iota((8, 128), 0)
    rows = [field[8 * k : 8 * k + 8] for k in range(8)]
    up = [pltpu.roll(value, 7, 0) for value in rows]
    down = [pltpu.roll(value, 1, 0) for value in rows]
    moved = []
    for k in range(8):
        above = jnp.where(sub == 7, up[k + 1], up[k]) if k < 7 else jnp.where(sub >= 1, rows[7], up[7])
        below = jnp.where(sub == 0, down[k - 1] if k else rows[0], down[k])
        moved.append(above + below)
    return jnp.concatenate(moved, axis=0)


def transported(field, along, momentum):
    return (
        0.4 * field
        + 0.15 * (along[:, :128] + levels_moved(field))
        + momentum * along[:, 128:]
    )


def condensed(heat, water, wet, saturation):
    cond = wet * jnp.maximum(water - 0.5 * heat - saturation, 0.0)
    return heat + 0.8 * cond, water - cond


def kernel(
    dyn, crm, mask, span, sums_in, matrices, along_in, spread_in, means_in, pick_in,
    hr, part_out, crm_out,
    xin, xb, mk, sp, sums, mat, along, spread, means, pick,
    spans, xs, ys, wt, cat, og, ar, rs, rt, dh, dr, hs, ob, od, place, post,
    load_sem, store_sem, go_sem, come_sem, tile_sem,
):
    p, r = lax.axis_index("blk"), lax.axis_index("row")
    rows, blocks = lax.axis_size("row"), lax.axis_size("blk")
    barrier = pltpu.get_barrier_semaphore()

    def far_first(k):
        return lax.rem(r + 16 + (1 - 2 * (k & 1)) * ((k + 1) >> 1), rows)

    def greet(k, carry):
        pl.semaphore_signal(barrier, inc=1, device_id=(p, far_first(k)), device_id_type=MESH)
        return carry

    lax.fori_loop(0, rows - 1, greet, None, unroll=True)
    around = [
        (lax.rem(p + blocks - dx, blocks), lax.rem(r + rows - dy, rows)) for dx, dy in SLOTS
    ]
    for slot in range(2, 8):
        pl.semaphore_signal(barrier, inc=1, device_id=around[slot], device_id_type=MESH)

    loads = [
        pltpu.make_async_copy(source, target, load_sem.at[k])
        for k, (source, target) in enumerate(
            ((span, sp), (sums_in, sums), (dyn, xin), (crm, xb), (mask, mk), (along_in, along),
             (spread_in, spread), (means_in, means), (matrices, mat), (pick_in, pick))
        )
    ]
    for load in loads[:3]:
        load.start()

    cat[...] = jnp.zeros_like(cat)
    spans[...] = jnp.zeros_like(spans)

    def table(k, lines=128):
        at = (0, 256, 512, 768, 1024, 1024 + 2 * HALO)[k]
        return mat[at : at + lines], mat[at + lines : at + 2 * lines]

    loads[0].wait()
    spans[0:1, 0:32] = sp[...].astype(F32)
    named = spans[...]
    named = named + pltpu.roll(named, 32, 1)
    named = named + pltpu.roll(named, 64, 1)
    lane, line = iota((32, 128), 1), iota((32, 128), 0)
    across = jnp.broadcast_to(named[0:1, :], (32, 128))
    down = jnp.sum(jnp.where(lane == line, across, 0.0), axis=1, keepdims=True)
    earlier = jnp.where((down == across) & (line < (lane & 31)), 1.0, 0.0)
    position = 2.0 * named[0:1, :] + jnp.sum(earlier, axis=0, keepdims=True)
    lane, line = iota((128, 128), 1), iota((128, 128), 0)
    wanted = (2 * line - (line & 3)).astype(F32)
    offered = 4.0 * jnp.broadcast_to(position, (128, 128)) + (lane >> 5).astype(F32)
    send_to = jnp.concatenate(
        [jnp.where(offered - 4.0 * s == wanted, 1.0, 0.0) for s in range(2)], axis=1
    ).astype(BF16)

    loads[1].wait()
    loads[2].wait()
    for load in loads[3:6]:
        load.start()
    for field in range(3):
        cat[32 * field : 32 * field + 32, 0:LEV] = dot_split((sums[0:32], sums[32:64]), xin[field])
    first = jnp.where(lane < CRM_LEV, cat[...], 0.0)
    high, low = halves(jnp.concatenate([first, pltpu.roll(first, 64, 1)], axis=0))
    sent = dot(send_to, jnp.concatenate([high, low], axis=1))
    og[...] = (sent[:, :128] + sent[:, 128:]).reshape(32, 4, 128)

    pl.semaphore_wait(barrier, rows - 1 + 6)

    def profile_copy(target):
        return pltpu.make_async_remote_copy(
            src_ref=og.at[target], dst_ref=ar.at[r], send_sem=go_sem.at[0],
            recv_sem=tile_sem.at[lax.div(r, 2 * TILES)], device_id=(p, target), device_id_type=MESH,
        )

    def send_profile(k, carry):
        profile_copy(far_first(k)).start()
        return carry

    lax.fori_loop(0, rows - 1, send_profile, None, unroll=True)
    ar[r] = og[r]

    for load in loads[6:]:
        load.start()

    for k in range(3, 6):
        loads[k].wait()
    row = iota((64, 128), 0)
    saturation = 0.5 - row.astype(F32) / CRM_LEV
    rest = jnp.zeros((64 - CRM_LEV, 128), F32)

    def begin(group, carry):
        first = pl.multiple_of(group * TILES, TILES)
        state = []
        for t in range(TILES):
            at = pl.ds(pl.multiple_of(128 * (first + t), 128), 128)
            wt[first + t] = jnp.concatenate([0.5 * mk[:, at].astype(F32), rest], axis=0)
            for f in range(3):
                state.append(jnp.concatenate([xb[f, :, at].astype(F32), rest], axis=0))
        shifted = dot(jnp.concatenate(state, axis=0).astype(BF16), along[0:128, :])
        for t in range(TILES):
            momentum = -0.1 * state[3 * t + 2]
            for f in range(3):
                line = 64 * (3 * t + f)
                moved = transported(state[3 * t + f], shifted[line : line + 64], momentum)
                ys[first + t, 64 * f : 64 * f + 64, :] = moved
        start = jnp.concatenate(
            [jnp.concatenate(state[3 * t : 3 * t + 3], axis=1) for t in range(TILES)], axis=0
        )
        mean = slot_means(means[...], start.astype(BF16))
        for t in range(TILES):
            part = mean[:, 64 * t : 64 * t + 64]
            xs[first + t] = jnp.concatenate([part[0:8], part[8:16]], axis=1)
        return carry

    loads[7].wait()
    lax.fori_loop(0, GROUPS, begin, None)
    loads[6].wait()

    def all_of(source, target, k):
        return pltpu.make_async_remote_copy(
            src_ref=source.at[pl.ds(0, 31)], dst_ref=target.at[pl.ds(0, 31)],
            send_sem=go_sem.at[k], recv_sem=come_sem.at[k],
            device_id=(p, lax.rem(r + 1, rows)), device_id_type=MESH,
        )

    def tendency_copy(target):
        return pltpu.make_async_remote_copy(
            src_ref=rs.at[target], dst_ref=rt.at[r], send_sem=go_sem.at[2],
            recv_sem=come_sem.at[2], device_id=(p, target), device_id_type=MESH,
        )

    mine = lax.div(r, 2 * TILES)

    def finish(k, carry):
        late = k >> 1
        group = (3 - k) * (1 - late) + (k - 2) * late
        first = pl.multiple_of(group * TILES, TILES)
        near = ar.at[pl.ds(2 * first, 2 * TILES)]

        def wait(count):
            due = ar.at[pl.ds(2 * first, count)]
            pltpu.make_async_copy(due, due, tile_sem.at[group]).wait()

        pl.when(group != mine)(lambda: wait(2 * TILES))
        pl.when(group == mine)(lambda: wait(2 * TILES - 1))
        near = 0.3 * near[...].reshape(8 * TILES, 128)
        parts = [part.astype(F32) for part in (*halves(near), *halves(pltpu.roll(near, 64, 1)))]
        near = jnp.concatenate(
            [parts[k][8 * t : 8 * t + 8] for t in range(TILES) for k in (0, 2, 1, 3)], axis=0
        ).T[0:64]
        near = [near] + [pltpu.roll(near, 128 - 32 * t, 1) for t in range(1, TILES)]
        pulled = dot(jnp.concatenate(near, axis=0).astype(BF16), spread[...])
        pulled = [
            [pulled[64 * t : 64 * t + 64, 128 * f : 128 * f + 128] for f in range(3)]
            for t in range(TILES)
        ]
        fields = []
        for t in range(TILES):
            one = [ys[first + t, 64 * f : 64 * f + 64, :] + pulled[t][f] for f in range(3)]
            one[0], one[1] = condensed(one[0], one[1], wt[first + t], saturation)
            fields.append(one)
        both = [jnp.concatenate(halves(value), axis=1) for one in fields for value in one]
        shifted = dot(jnp.concatenate(both, axis=0), along[...])
        change = []
        for t in range(TILES):
            at = pl.ds(pl.multiple_of(128 * (first + t), 128), 128)
            one = fields[t]
            momentum = -0.1 * one[2]
            two = []
            for f in range(3):
                line = 64 * (3 * t + f)
                moved = transported(one[f], shifted[line : line + 64], momentum)
                two.append(moved + pulled[t][f])
            two[0], two[1] = condensed(two[0], two[1], wt[first + t], saturation)
            parts = []
            for f in range(3):
                parts.append(halves(two[f]))
                ob[f, :, at] = parts[f][0][0:CRM_LEV]
            change += [jnp.concatenate([part[h] for part in parts], axis=1) for h in range(2)]
        mean = [
            slot_means(means[...], jnp.concatenate(change[2 * t : 2 * t + 2], axis=0))
            for t in range(TILES)
        ]
        for t in range(TILES):
            part = mean[t] + pltpu.roll(mean[t], 64, 1)
            message = jnp.where(iota((8, 128), 1) < 64, part[0:8], part[8:16]) - xs[first + t]
            for pair in range(2):
                rs[2 * (first + t) + pair] = message[4 * pair : 4 * pair + 4]
        for k in range(2 * TILES):
            target = 2 * first + k
            pl.when(target != r)(tendency_copy(target).start)
        return carry

    lax.fori_loop(0, GROUPS, finish, None)
    rt[r] = rs[r]

    store = pltpu.make_async_copy(ob, crm_out, store_sem.at[0])
    store.start()

    loads[8].wait()
    for field in range(4):
        dh[:, 128 * field : 128 * field + LEV] = dot_split(table(0), xin[field])
    state_copies = []
    for slot in range(8):
        at = pl.ds(STATE_AT[slot], STATE_ROWS[slot])
        state_copies.append(
            pltpu.make_async_remote_copy(
                src_ref=dh.at[at], dst_ref=dr.at[at], send_sem=go_sem.at[1],
                recv_sem=come_sem.at[1], device_id=around[slot], device_id_type=MESH,
            )
        )
        state_copies[-1].start()

    loads[9].wait()
    lane, line = iota((32, 128), 1), iota((32, 128), 0)
    home = jnp.sum(
        jnp.where(lane == line, jnp.broadcast_to(position, (32, 128)), 0.0), axis=1, keepdims=True
    )
    code = (lane >> 2).astype(F32)
    match = jnp.concatenate(
        [jnp.where(home - s == 2.0 * code, 1.0, 0.0) for s in range(2)], axis=1
    )
    lane = iota((32, 256), 1)
    for field in range(3):
        place[32 * field : 32 * field + 32, :] = jnp.where((lane & 3) == field, match, 0.0).astype(BF16)
    match = match.astype(BF16)
    for h in range(2):
        for half, piece in enumerate(table(4 + h, HALO)):
            at = (2 * half + h) * HALO
            post[at : at + HALO, :] = (
                pick[...] * dot(piece[:, 0:32], match)
            ).astype(BF16)

    for field in range(4):
        od[field, :, 0:LEV] = dot_split(table(1), xin[field])

    all_of(rs, rt, 2).wait_recv()
    given = rt[...].reshape(128, 128)
    lane = iota((128, 128), 1)
    given = [jnp.where(lane < CRM_LEV, value, 0.0) for value in (given, pltpu.roll(given, 64, 1))]
    given = jnp.concatenate(halves(jnp.concatenate(given, axis=0)), axis=1)
    sent = dot(post[0 : 2 * HALO, :], given)
    low = dot(post[2 * HALO : 4 * HALO, :], given[:, 0:128])
    sent = sent[:, 0:128] + sent[:, 128:256] + low
    sent = [sent[0:HALO], sent[HALO:]]
    hs[...] = sent[0] + pltpu.roll(sent[1], 64, 1)
    for slot in (4, 5, 6, 7, 0, 1, 2, 3):
        at = pl.ds(CELL_AT[slot], CELL_ROWS[slot])
        pltpu.make_async_remote_copy(
            src_ref=hs.at[at], dst_ref=hr.at[at], send_sem=go_sem.at[3],
            recv_sem=come_sem.at[3], device_id=around[slot], device_id_type=MESH,
        ).start()
    cells = dot(place[...], given)
    cells = cells[:, 0:128] + cells[:, 128:256]
    own = table(3)
    own = own[0][:, 0:32], own[1][:, 0:32]
    for field in range(3):
        od[field, :, 0:LEV] += dot_split(own, cells[32 * field : 32 * field + 32])[:, 0:LEV]

    pltpu.make_async_remote_copy(
        src_ref=dh, dst_ref=dr, send_sem=go_sem.at[1], recv_sem=come_sem.at[1],
        device_id=around[0], device_id_type=MESH,
    ).wait_recv()
    for field in range(4):
        od[field, :, 0:LEV] += dot_split(table(2), dr[:, 128 * field : 128 * field + 128])[:, 0:LEV]

    halo_copy = pltpu.make_async_remote_copy(
        src_ref=hs, dst_ref=hr, send_sem=go_sem.at[3],
        recv_sem=come_sem.at[3], device_id=around[0], device_id_type=MESH,
    )
    part = pltpu.make_async_copy(od, part_out, store_sem.at[1])
    part.start()
    halo_copy.wait_recv()
    all_of(og, ar, 0).wait_send()
    all_of(rs, rt, 2).wait_send()
    pltpu.make_async_remote_copy(
        src_ref=dh, dst_ref=dr, send_sem=go_sem.at[1], recv_sem=come_sem.at[1],
        device_id=around[0], device_id_type=MESH,
    ).wait_send()
    halo_copy.wait_send()
    store.wait()
    part.wait()


def last_kernel(came_in, part, arrive, crm_in, dyn_out, crm_out, od, sem):
    crm = pltpu.make_async_copy(crm_in, crm_out, sem.at[0])
    crm.start()
    stores = [pltpu.make_async_copy(od.at[f], dyn_out.at[f], sem.at[1 + f]) for f in range(4)]
    od[3] = part[3, :, 0:LEV]
    stores[3].start()
    lane = iota((HALO, 128), 1)
    came = came_in[...]
    came = [jnp.where(lane < 64, value, 0.0) for value in (came, pltpu.roll(came, 64, 1))]
    came = jnp.concatenate(came + [jnp.zeros((256 - 2 * HALO, 128), F32)], axis=0)
    came = jnp.concatenate(halves(came), axis=1)
    taken = dot(arrive[...], came)
    for f in range(3):
        high, low = taken[128 * f : 128 * f + 128], taken[384 + 128 * f : 512 + 128 * f]
        od[f] = part[f, :, 0:LEV] + (high[:, 0:128] + high[:, 128:256] + low[:, 0:128])[:, 0:LEV]
        stores[f].start()
    crm.wait()
    for store in stores:
        store.wait()


def per_device(dyn_state, crm_state, cloud_mask, span_of):
    *consts, arrive = (jnp.asarray(value) for value in tables())
    vmem = pltpu.VMEM
    scratch = [
        vmem((4, 128, LEV), F32), vmem((3, CRM_LEV, 2048), BF16), vmem((CRM_LEV, 2048), jnp.int32),
        vmem((1, 32), jnp.int32),
    ]
    scratch += [vmem(value.shape, value.dtype) for value in consts]
    scratch += [
        vmem((8, 128), F32),
        vmem((16, 8, 128), F32), vmem((16, 192, 128), F32), vmem((16, 64, 128), F32),
        vmem((128, 128), F32),
        vmem((32, 4, 128), F32), vmem((32, 4, 128), F32),
        vmem((32, 4, 128), F32), vmem((32, 4, 128), F32),
        vmem((128, 512), F32), vmem((128, 512), F32),
        vmem((HALO, 128), F32),
        vmem((3, CRM_LEV, 2048), BF16), vmem((4, 128, 128), F32),
        vmem((96, 256), BF16), vmem((4 * HALO, 256), BF16),
        pltpu.SemaphoreType.DMA((10,)), pltpu.SemaphoreType.DMA((2,)),
        pltpu.SemaphoreType.DMA((4,)), pltpu.SemaphoreType.DMA((4,)), pltpu.SemaphoreType.DMA((GROUPS,)),
    ]
    nodes = dyn_state.transpose(0, 2, 3, 1).reshape(4, 128, LEV)
    operands = (nodes, crm_state, cloud_mask, span_of.T, *consts)
    anywhere = pl.BlockSpec(memory_space=pl.ANY)
    came, part, crm = pl.pallas_call(
        kernel,
        out_shape=(
            vmem((HALO, 128), F32), vmem((4, 128, 128), F32), vmem((3, CRM_LEV, 2048), BF16)
        ),
        in_specs=[anywhere] * 10,
        out_specs=[anywhere] * 3,
        scratch_shapes=scratch,
        compiler_params=pltpu.CompilerParams(
            collective_id=0, has_side_effects=True, vmem_limit_bytes=40 * 2**20
        ),
        name="physics_step",
    )(*(pltpu.with_memory_space_constraint(value, pltpu.HBM) for value in operands))
    near = pl.BlockSpec(memory_space=pltpu.VMEM)
    dyn, crm = pl.pallas_call(
        last_kernel,
        out_shape=(
            pltpu.HBM((4, 128, LEV), F32), pltpu.HBM((3, CRM_LEV, 2048), BF16)
        ),
        in_specs=[near, near, near, anywhere],
        out_specs=[anywhere] * 2,
        scratch_shapes=[
            vmem((4, 128, LEV), F32), pltpu.SemaphoreType.DMA((5,))
        ],
        compiler_params=pltpu.CompilerParams(vmem_limit_bytes=8 * 2**20),
        name="last_step",
    )(came, part, arrive, crm)
    return dyn.reshape(4, 16, 8, LEV).transpose(0, 3, 1, 2), crm


def solution(mesh):
    return jax.shard_map(
        per_device,
        mesh=mesh,
        in_specs=(
            P(None, None, "blk", "row"),
            P(None, None, ("blk", "row")),
            P(None, ("blk", "row")),
            P(("blk", "row"), None),
        ),
        out_specs=(P(None, None, "blk", "row"), P(None, None, ("blk", "row"))),
        check_vma=False,
    )
```
